128 devices in a mesh: pair: 32 (over z_hi, y, x), ao: 4 (over z_lo, core).
Axes of the slice: x: 4, y: 4, z: 4 (z_hi: 2, z_lo: 2; z = z_hi * 2 + z_lo), core: 2. Of those that a mesh axis runs over, the one named last changes fastest.
Arguments:
- amps_ao: bfloat16 [1024, 65536], P('pair'), may hold values from -6 to 6
- integrals: bfloat16 [65536, 16384], P('pair', 'ao'), may hold values from -0.0234375 to 0.0234375
- tile_sizes: int32 [256], P('pair'), may hold values from 1 to 256, 39321 in all
- pair_list: int32 [1024, 2], P('pair'), may hold values from 0 to 199, as said below
- partner: int32 [1024], replicated, may hold values from 0 to 1023, as said below
- occ_energy: float32 [200], replicated, may hold values from -2 to -0.3
- vir_energy: float32 [128], replicated, may hold values from 0.2 to 3
- amplitudes: float32 [1024, 16384], P('pair', 'ao'), may hold values from -3 to 3
- other_terms: float32 [1024, 16384], P('pair', 'ao'), may hold values from -6 to 6
Outputs:
- residual: float32 [1024, 16384], P('pair', 'ao')
- updated: float32 [1024, 16384], P('pair', 'ao')
The draws below stay inside these ranges and needn't reach their ends.
Inputs may be any that keep to these rules, and one draw needn't show every extreme that they name: `pair_list`: every pair i, j has i != j, appears once, and its pair j, i appears too. partner is an involution without fixed points, and pair_list[partner[p]] is pair_list[p] reversed. With B = 32, partner[p] // 32 equals (p // 32 + B // 2) mod B.
All inputs are finite; a program needn't handle non-finite values. No bound on the sum of `tile_sizes` on one device may be relied on, other than what follows from the above.
Results may differ from the reference program's by a relative error of at most 0.0003.
Values may be sent and summed in bfloat16 or wider, within the bound.
A program may use at most 192 MiB of HBM per device.

```python
import math
import jax
import jax.numpy as jnp
import numpy as np

NOCC = 200
NL = 128
TILE = 256
SLOTS = 32
PAIRS = 1024
Q = 65536


def pair_layout(base_key):
    half_count = PAIRS // 2
    device_count = PAIRS // SLOTS
    half_devices = device_count // 2
    rounds = half_count // NOCC + 1
    gaps = jax.random.permutation(jax.random.fold_in(base_key, 11), NOCC // 2 - 2)[:rounds] + 1
    occ_perm = jax.random.permutation(jax.random.fold_in(base_key, 12), NOCC)
    occ_perm = (occ_perm - occ_perm[0] + NOCC - 1) % NOCC
    serial = jnp.arange(half_count, dtype=jnp.int32)
    lower = occ_perm[serial % NOCC]
    upper = (lower + gaps[serial // NOCC]) % NOCC
    order = jax.random.permutation(jax.random.fold_in(base_key, 13), half_count)
    flips = jax.random.randint(jax.random.fold_in(base_key, 14), (half_count,), 0, 2)
    lower = lower[order]
    upper = upper[order]
    first_occ = jnp.where(flips == 1, upper, lower).astype(jnp.int32)
    second_occ = jnp.where(flips == 1, lower, upper).astype(jnp.int32)
    slot_keys = jax.random.split(jax.random.fold_in(base_key, 15), half_devices)
    slot_perms = jax.vmap(lambda k: jax.random.permutation(k, SLOTS))(slot_keys).astype(jnp.int32)
    home_dev = serial // SLOTS
    home_slot = serial % SLOTS
    mirror = ((home_dev + half_devices) * SLOTS + slot_perms[home_dev, home_slot]).astype(jnp.int32)
    slot_pairs = jnp.zeros((PAIRS, 2), jnp.int32)
    slot_pairs = slot_pairs.at[serial, 0].set(first_occ).at[serial, 1].set(second_occ)
    slot_pairs = slot_pairs.at[mirror, 0].set(second_occ).at[mirror, 1].set(first_occ)
    partner_slot = jnp.zeros((PAIRS,), jnp.int32)
    partner_slot = partner_slot.at[serial].set(mirror).at[mirror].set(serial)
    return (slot_pairs, partner_slot)


def draw_pair_list(key, part):
    layout = pair_layout(key)
    return layout[0]


def draw_partner(key, part):
    layout = pair_layout(key)
    return layout[1]


def level_of(stream_key, dims, shards, smallest, high):
    loudness, own = 1.0, jax.random.fold_in(stream_key, 6)
    for dim, parts in shards:
        steps = jnp.exp(jax.random.uniform(jax.random.fold_in(own, dim), (parts,), jnp.float32, smallest / len(shards), high / len(shards)))
        loudness = loudness * jnp.repeat(steps, dims[dim] // parts).reshape([-1 if axis == dim else 1 for axis in range(len(dims))])
    return loudness


def length_profile(number_of, total, bound, skew):
    loads = [(1 << 20) // math.isqrt(standing ** skew) + 1 for standing in range(2, number_of + 1)]
    rest, holding = total - bound - (number_of - 1), [1] * (number_of - 1)
    while rest > 0:
        candidates = [i for i in range(number_of - 1) if holding[i] < bound]
        whole, left = sum([loads[i] for i in candidates]), rest
        for i in candidates:
            addition = min(bound - holding[i], max(1, left * loads[i] // whole), rest)
            holding[i] = holding[i] + addition
            rest = rest - addition
    return np.array([bound] + holding)


def ragged_sizes(stream_key, amount, total, reach, skew):
    if amount == 2:
        one = jax.random.randint(stream_key, (), max(1, total - reach), min(reach, total - 1) + 1)
        return jnp.stack([one, total - one])
    lengths = jnp.asarray(length_profile(amount, total, reach, skew), jnp.int32)
    pairs = (amount - 1) // 2
    giver, receiver = lengths[1:1 + 2 * pairs:2], lengths[2:2 + 2 * pairs:2]
    margin = jnp.minimum(giver - 1, reach - receiver)
    shifted = jax.random.randint(jax.random.fold_in(stream_key, 1), (pairs,), 0, 1 << 20) % (margin + 1)
    lengths = lengths.at[1:1 + 2 * pairs:2].set(giver - shifted).at[2:2 + 2 * pairs:2].set(receiver + shifted)
    return lengths[jax.random.permutation(jax.random.fold_in(stream_key, 2), amount)]


def noise(stream_key, extent, scale, reach, cuts=(), kind=jnp.bfloat16):
    level = level_of(stream_key, extent, cuts, -0.22, 0.18) if cuts else 1.0
    entries = jax.random.normal(stream_key, extent, jnp.float32) * scale * level
    return jnp.minimum(jnp.maximum(entries, -reach), reach).astype(kind)


def setup_inputs(seed: int = 0) -> dict:
    keys = jax.random.split(jax.random.key(seed), 10)
    return {
        "amps_ao": noise(keys[0], (PAIRS, Q), 1.0, 6.0, ((0, 32),)),
        "integrals": noise(keys[1], (Q, NL * NL), Q ** -0.5, 0.0234375, ((0, 32), (1, 4))),
        "tile_sizes": ragged_sizes(keys[2], Q // TILE, Q * 3 // 5, TILE, 2).astype(jnp.int32),
        "pair_list": draw_pair_list(jax.random.fold_in(keys[9], 71), 0),
        "partner": draw_partner(jax.random.fold_in(keys[9], 71), 0),
        "occ_energy": jnp.clip(jax.random.uniform(keys[5], (NOCC,), jnp.float32, -2.0, -0.3), -2.0, -0.3),
        "vir_energy": jnp.clip(jax.random.uniform(keys[6], (NL,), jnp.float32, 0.2, 3.0), 0.2, 3.0),
        "amplitudes": noise(keys[7], (PAIRS, NL * NL), 0.2, 3.0, ((0, 32), (1, 4)), jnp.float32),
        "other_terms": noise(keys[8], (PAIRS, NL * NL), 1.0, 6.0, ((0, 32), (1, 4)), jnp.float32),
    }


def reference(amps_ao, integrals, tile_sizes, pair_list, partner, occ_energy, vir_energy, amplitudes, other_terms):
    live_rows = jnp.arange(TILE)[None, :] < tile_sizes[:, None]
    screened = jnp.where(live_rows.reshape(-1, 1), integrals, jnp.zeros((), jnp.bfloat16))
    ladder = jnp.dot(amps_ao, screened, preferred_element_type=jnp.float32).reshape(PAIRS, NL, NL)
    swapped = jnp.swapaxes(ladder[partner], 1, 2)
    symmetric = 0.5 * (ladder + swapped)
    occ_sum = occ_energy[pair_list[:, 0]] + occ_energy[pair_list[:, 1]]
    denominator = vir_energy[None, :, None] + vir_energy[None, None, :] - occ_sum[:, None, None]
    amp_cube = amplitudes.reshape(PAIRS, NL, NL)
    residual = other_terms.reshape(PAIRS, NL, NL) + symmetric - denominator * amp_cube
    updated = amp_cube + residual / denominator
    return residual.reshape(PAIRS, NL * NL), updated.reshape(PAIRS, NL * NL)
```

```python
import functools

import jax
import jax.numpy as jnp
from jax import lax
from jax.experimental import pallas as pl
from jax.experimental.pallas import tpu as pltpu
from jax.sharding import PartitionSpec as P

NOCC = 200
NL = 128
TILE = 256
ROWS = 32
SLAB = 2048
HALF = SLAB // 2
COLS = 4096
C = 512
NK = COLS // 2 // C
MESH = pl.DeviceIdType.MESH

STEPS = 32760.0
LIMIT = (288.0, 1152.0, 4608.0)
FLOOR = (2.0**-12, 2.0**-11, 2.0**-10)
OCTAVES = (20.1699, 21.1699, 22.1699)


def encode(value, stage):
    level = jnp.log2(1.0 + jnp.abs(value) * (1.0 / FLOOR[stage])) * (STEPS / OCTAVES[stage])
    level = jnp.where(value < 0.0, -level, level)
    return jnp.round(level).astype(jnp.int32).astype(jnp.int16)


def decode(code, stage):
    level = code.astype(jnp.int32).astype(jnp.float32)
    size = (jnp.exp2(jnp.abs(level) * (OCTAVES[stage] / STEPS)) - 1.0) * FLOOR[stage]
    return jnp.where(level < 0.0, -size, size)


def ladder_kernel(
    amps, integrals, sizes, out,
    a, b, total, own1, out1, in1, out2, in2, out3, in3, mask,
    amp_send, amp_recv, mate_send, mate_recv, own_sem, b_sem,
    send1, recv1, send2, recv2, send3, recv3,
):
    pair, ao = lax.axis_index("pair"), lax.axis_index("ao")
    zh, y, x = pair // 16, (pair // 4) % 4, pair % 4
    zl, core = ao // 2, ao % 2
    mate = (pair, zl * 2 + 1 - core)
    across = (((zh + 1) % 2) * 16 + y * 4 + x, ao)

    def offset(j):
        return j // 16, (j // 4) % 4, j % 4

    def target(j):
        dz, dy, dx = offset(j)
        there = ((zh + dz) % 2) * 16 + ((y + dy) % 4) * 4 + (x + dx) % 4
        return there, ((zl + dz) % 2) * 2 + core

    def ring(part, j):
        if part == 0:
            return zh * 16 + y * 4 + (x + j) % 4, ao
        return zh * 16 + ((y + j) % 4) * 4 + x, ao

    barrier = pltpu.get_barrier_semaphore()

    def greet(j, carry):
        pl.semaphore_signal(barrier, inc=1, device_id=target(j), device_id_type=MESH)
        return carry

    lax.fori_loop(1, 32, greet, 0)
    for peer in (mate, across):
        pl.semaphore_signal(barrier, inc=1, device_id=peer, device_id_type=MESH)
    pl.semaphore_wait(barrier, 33)

    def rows_of(sx, sy, sz, half):
        return a.at[sx, sy, pl.ds(sz * ROWS, ROWS), pl.ds(half * HALF, HALF)]

    def amp_copy(j):
        there, their_ao = target(j)
        return pltpu.make_async_remote_copy(
            src_ref=amps.at[:, pl.ds(there * SLAB + core * HALF, HALF)],
            dst_ref=rows_of(x, y, zh, core),
            send_sem=amp_send.at[j - 1], recv_sem=amp_recv.at[j - 1],
            device_id=(there, their_ao), device_id_type=MESH)

    def arrived(j, half, send, recv):
        dz, dy, dx = offset(j)
        block = rows_of((x + 4 - dx) % 4, (y + 4 - dy) % 4, (zh + dz) % 2, half)
        return pltpu.make_async_remote_copy(
            src_ref=block, dst_ref=block, send_sem=send.at[j - 1], recv_sem=recv.at[j - 1],
            device_id=mate, device_id_type=MESH)

    def start_amp(j, carry):
        amp_copy(j).start()
        return carry

    lax.fori_loop(1, 32, start_amp, 0)
    own_copy = pltpu.make_async_copy(
        amps.at[:, pl.ds(pair * SLAB, SLAB)], a.at[x, y, pl.ds(zh * ROWS, ROWS), :], own_sem)
    own_copy.start()

    def b_copy(i):
        cols = pl.ds(i * C, C)
        return pltpu.make_async_copy(integrals.at[:, cols], b.at[:, cols], b_sem.at[i])

    for k in range(NK):
        b_copy(k).start()
        b_copy(NK + k).start()

    lane = lax.broadcasted_iota(jnp.int32, (16, TILE), 1)
    for t in range(SLAB // TILE):
        mask[:, t * TILE:(t + 1) * TILE] = jnp.where(lane < sizes[t], 1.0, 0.0).astype(jnp.bfloat16)

    def forward(j, carry):
        arrived(j, core, amp_send, amp_recv).wait_recv()
        arrived(j, core, mate_send, mate_recv).start()
        return carry

    lax.fori_loop(1, 32, forward, 0)

    def settle(j, carry):
        arrived(j, 1 - core, mate_send, mate_recv).wait_recv()
        arrived(j, core, mate_send, mate_recv).wait_send()
        amp_copy(j).wait_send()
        return carry

    lax.fori_loop(1, 32, settle, 0)
    own_copy.wait()

    def screen(i, carry):
        for r in range(4):
            rows = pl.ds(r * 16, 16)
            a[i // 4, i % 4, rows, :] = a[i // 4, i % 4, rows, :] * mask[...]
        return carry

    lax.fori_loop(0, 16, screen, 0)

    def copy1(part, k, j):
        return pltpu.make_async_remote_copy(
            src_ref=out1.at[part, k, j], dst_ref=in1.at[part, k, j],
            send_sem=send1.at[part, k, j], recv_sem=recv1.at[part, k, j],
            device_id=ring(part, j + 1), device_id_type=MESH)

    def copy2(part, k, j):
        return pltpu.make_async_remote_copy(
            src_ref=out2.at[part, k, j], dst_ref=in2.at[part, k, j],
            send_sem=send2.at[part, k, j], recv_sem=recv2.at[part, k, j],
            device_id=ring(1 - part, j + 1), device_id_type=MESH)

    def copy3(part, k):
        return pltpu.make_async_remote_copy(
            src_ref=out3.at[part, k], dst_ref=in3.at[part, k],
            send_sem=send3.at[part, k], recv_sem=recv3.at[part, k],
            device_id=across, device_id_type=MESH)

    def block_of(part, d):
        block = total[d] if part == 0 else total[:, d]
        return block.reshape(256, C)

    def multiply(k, carry):
        for part in range(2):
            i = part * NK + k
            b_copy(i).wait()
            total[...] = jnp.dot(
                a[...].reshape(1024, SLAB), b[:, pl.ds(pl.multiple_of(i * C, C), C)],
                preferred_element_type=jnp.float32).reshape(4, 4, 64, C)
            here = x if part == 0 else y

            def push(j, inner):
                out1[part, k, j] = encode(block_of(part, (here + j + 1) % 4), 0)
                copy1(part, k, j).start()
                return inner

            lax.fori_loop(0, 3, push, 0)
            own1[part, k] = block_of(part, here)
        return carry

    lax.fori_loop(0, NK, multiply, 0)

    def reduce1(k, carry):
        for part in range(2):
            for j in range(3):
                copy1(part, k, j).wait_recv()
            there = y if part == 0 else x

            def summed(d):
                rows = pl.ds(pl.multiple_of(d * 64, 64), 64)
                value = own1[part, k, rows, :]
                for j in range(3):
                    value = value + decode(in1[part, k, j, rows, :], 0)
                return value

            def push(j, inner):
                out2[part, k, j] = encode(summed((there + j + 1) % 4), 1)
                copy2(part, k, j).start()
                return inner

            lax.fori_loop(0, 3, push, 0)
            rows = pl.ds(pl.multiple_of(there * 64, 64), 64)
            own1[part, k, rows, :] = summed(there)
        return carry

    lax.fori_loop(0, NK, reduce1, 0)

    def reduce2(k, carry):
        for part in range(2):
            there = y if part == 0 else x
            rows = pl.ds(pl.multiple_of(there * 64, 64), 64)
            value = own1[part, k, rows, :]
            for j in range(3):
                copy2(part, k, j).wait_recv()
                value = value + decode(in2[part, k, j], 1)
            out3[part, k] = encode(value, 2)
            copy3(part, k).start()
            own1[part, k, rows, :] = value
        return carry

    lax.fori_loop(0, NK, reduce2, 0)

    def finish(k, carry):
        for part in range(2):
            there = y if part == 0 else x
            rows = pl.ds(pl.multiple_of(there * 64, 64), 64)
            copy3(part, k).wait_recv()
            cols = pl.ds(pl.multiple_of((part * NK + k) * C, C), C)
            out[:, cols] = own1[part, k, rows, :] + decode(in3[part, k], 2)
            copy3(part, k).wait_send()
            for j in range(3):
                copy1(part, k, j).wait_send()
                copy2(part, k, j).wait_send()
        return carry

    lax.fori_loop(0, NK, finish, 0)


def ladder_rows(amps_ao, integrals, tile_sizes):
    sem = pltpu.SemaphoreType.DMA
    vmem = pltpu.VMEM
    return pl.pallas_call(
        ladder_kernel,
        out_shape=jax.ShapeDtypeStruct((64, COLS), jnp.float32),
        in_specs=[
            pl.BlockSpec(memory_space=pl.ANY),
            pl.BlockSpec(memory_space=pl.ANY),
            pl.BlockSpec(memory_space=pltpu.SMEM),
        ],
        out_specs=pl.BlockSpec(memory_space=pltpu.VMEM),
        scratch_shapes=[
            vmem((4, 4, 64, SLAB), jnp.bfloat16),
            vmem((SLAB, COLS), jnp.bfloat16),
            vmem((4, 4, 64, C), jnp.float32),
            vmem((2, NK, 256, C), jnp.float32),
            vmem((2, NK, 3, 256, C), jnp.int16),
            vmem((2, NK, 3, 256, C), jnp.int16),
            vmem((2, NK, 3, 64, C), jnp.int16),
            vmem((2, NK, 3, 64, C), jnp.int16),
            vmem((2, NK, 64, C), jnp.int16),
            vmem((2, NK, 64, C), jnp.int16),
            vmem((16, SLAB), jnp.bfloat16),
            sem((31,)), sem((31,)), sem((31,)), sem((31,)), sem, sem((2 * NK,)),
            sem((2, NK, 3)), sem((2, NK, 3)), sem((2, NK, 3)), sem((2, NK, 3)),
            sem((2, NK)), sem((2, NK)),
        ],
        compiler_params=pltpu.CompilerParams(
            collective_id=0, has_side_effects=True, vmem_limit_bytes=60 << 20),
        cost_estimate=pl.CostEstimate(
            flops=2 * 1024 * SLAB * COLS, bytes_accessed=24 << 20, transcendentals=0),
        name="ladder",
    )(amps_ao, integrals, tile_sizes)


def local(
    amps_ao,
    integrals,
    tile_sizes,
    pair_list,
    partner,
    occ_energy,
    vir_energy,
    amplitudes,
    other_terms,
):
    slot_count = amps_ao.shape[0]
    col_count = integrals.shape[1]
    lam_rows = NL // lax.axis_size("ao")
    own_first = lax.axis_index("pair") * slot_count
    lam_first = lax.axis_index("ao") * lam_rows
    own_partner = lax.dynamic_slice_in_dim(partner, own_first, slot_count, 0)
    both = ladder_rows(amps_ao, integrals, tile_sizes)
    zh = lax.axis_index("pair") // 16
    ladder = lax.dynamic_slice_in_dim(both, zh * ROWS, ROWS, 0)
    neighbour = lax.dynamic_slice_in_dim(both, (1 - zh) * ROWS, ROWS, 0)
    mirrored = neighbour[own_partner % ROWS].reshape(slot_count, lam_rows, NL)
    arrived = lax.all_to_all(mirrored, "ao", split_axis=2, concat_axis=1, tiled=True)
    symmetric = 0.5 * (ladder + jnp.swapaxes(arrived, 1, 2).reshape(slot_count, col_count))
    occ_index = jnp.arange(NOCC, dtype=jnp.int32)
    picked = jnp.where(
        pair_list[:, :, None] == occ_index[None, None, :],
        occ_energy[None, None, :],
        jnp.float32(0.0),
    )
    occ_sum = jnp.sum(picked, axis=(1, 2))
    vir_rows = lax.dynamic_slice_in_dim(vir_energy, lam_first, lam_rows, 0)
    vir_pairs = (vir_rows[:, None] + vir_energy[None, :]).reshape(-1)
    denominator = vir_pairs[None, :] - occ_sum[:, None]
    residual = other_terms + symmetric - denominator * amplitudes
    updated = amplitudes + residual / denominator
    return (residual, updated)


def solution(mesh):
    in_specs = (
        P("pair", None),
        P("pair", "ao"),
        P("pair"),
        P("pair", None),
        P(),
        P(),
        P(),
        P("pair", "ao"),
        P("pair", "ao"),
    )
    out_specs = (P("pair", "ao"), P("pair", "ao"))
    return jax.shard_map(local, mesh=mesh, in_specs=in_specs, out_specs=out_specs, check_vma=False)
```

```python
import functools

import jax
import jax.numpy as jnp
from jax import lax
from jax.experimental import pallas as pl
from jax.experimental.pallas import tpu as pltpu
from jax.sharding import PartitionSpec as P

NL = 128
TILE = 256
ROWS = 32
SLAB = 2048
HALF = SLAB // 2
QUARTER = SLAB // 4
COLS = 4096
LAMS = 32
C = 512
NK = COLS // 2 // C
MESH = pl.DeviceIdType.MESH

STEPS = 32760.0
LIMIT = (288.0, 1152.0, 4608.0)
FLOOR = (2.0**-12, 2.0**-11, 2.0**-10)
OCTAVES = (20.1699, 21.1699, 22.1699)


def encode(value, stage):
    level = jnp.log2(1.0 + jnp.abs(value) * (1.0 / FLOOR[stage])) * (STEPS / OCTAVES[stage])
    level = jnp.where(value < 0.0, -level, level)
    return jnp.round(level).astype(jnp.int32).astype(jnp.int16)


def decode(code, stage):
    level = code.astype(jnp.int32).astype(jnp.float32)
    size = (jnp.exp2(jnp.abs(level) * (OCTAVES[stage] / STEPS)) - 1.0) * FLOOR[stage]
    return jnp.where(level < 0.0, -size, size)


def ladder_kernel(
    amps, integrals, sizes, out, turned,
    a, b, staged, total, own1, out1, in1, out2, in2, out3, in3, mask, rows3, out4, in4,
    b_sem, own_sem, half_send, half_recv, mate_send, mate_recv, z_send, z_recv, plane_send, plane_recv,
    group_send, group_recv, send1, recv1, send2, recv2, send3, recv3, send4, recv4,
):
    pair, ao = lax.axis_index("pair"), lax.axis_index("ao")
    zh, y, x = pair // 16, (pair // 4) % 4, pair % 4
    zl, core = ao // 2, ao % 2
    mate = (pair, zl * 2 + 1 - core)
    beside = (pair, (1 - zl) * 2 + core)
    opposite = ((1 - zh) * 16 + y * 4 + x, (1 - zl) * 2 + core)
    across = ((1 - zh) * 16 + y * 4 + x, ao)

    def in_plane(i):
        return ((y + i // 4) % 4) * 4 + (x + i % 4) % 4

    def ring(part, j):
        if part == 0:
            return zh * 16 + y * 4 + (x + j) % 4, ao
        return zh * 16 + ((y + j) % 4) * 4 + x, ao

    def remote(src, dst, send, recv, device):
        return pltpu.make_async_remote_copy(
            src_ref=src, dst_ref=dst, send_sem=send, recv_sem=recv,
            device_id=device, device_id_type=MESH)

    def each(first, last, body):
        def step(i, carry):
            body(i)
            return carry

        lax.fori_loop(first, last, step, 0)

    barrier = pltpu.get_barrier_semaphore()

    def greet(peer):
        pl.semaphore_signal(barrier, inc=1, device_id=peer, device_id_type=MESH)

    each(1, 16, lambda i: greet((zh * 16 + in_plane(i), ao)))
    for peer in (opposite, across, *((pair, (ao + i) % 4) for i in range(1, 4))):
        greet(peer)
    pl.semaphore_wait(barrier, 20)

    def half_cols(half):
        return pl.ds(pl.multiple_of(half * HALF, HALF), HALF)

    def half_copy(i):
        there = in_plane(i)
        first = (zh * 16 + there) * SLAB + core * HALF
        return remote(
            amps.at[:, pl.ds(pl.multiple_of(first, HALF), HALF)], a.at[0, x, y, :, half_cols(core)],
            half_send.at[i - 1], half_recv.at[i - 1], (zh * 16 + there, ao))

    def half_block(i, half):
        return a.at[0, (x + 4 - i % 4) % 4, (y + 4 - i // 4) % 4, :, half_cols(half)]

    def mate_copy(i, half):
        block = half_block(i, half)
        return remote(block, block, mate_send.at[i - 1], mate_recv.at[i - 1], mate)

    def quarter_cols(quarter):
        return pl.ds(pl.multiple_of(quarter * QUARTER, QUARTER), QUARTER)

    def z_copy(i):
        first = ((1 - zh) * 16 + i) * SLAB + ((1 - zl) * 2 + core) * QUARTER
        return remote(
            amps.at[:, pl.ds(pl.multiple_of(first, QUARTER), QUARTER)], staged.at[i],
            z_send.at[i], z_recv.at[i], opposite)

    def plane_copy(i):
        there = in_plane(i)
        return remote(
            staged.at[there], a.at[1, x, y, :, quarter_cols(ao)],
            plane_send.at[i - 1], plane_recv.at[i - 1], (zh * 16 + there, ao))

    def group_copy(kind, g, quarter, device):
        block = a.at[1, g, :, :, quarter_cols(quarter)]
        return remote(block, block, group_send.at[kind, g], group_recv.at[kind, g], device)

    each(1, 16, lambda i: half_copy(i).start())
    each(0, 16, lambda i: z_copy(i).start())
    own_copy = pltpu.make_async_copy(
        amps.at[:, pl.ds(pl.multiple_of(pair * SLAB, SLAB), SLAB)], a.at[0, x, y], own_sem)
    own_copy.start()

    def b_copy(t):
        cols = pl.ds(t * C, C)
        return pltpu.make_async_copy(integrals.at[:, cols], b.at[:, cols], b_sem.at[t])

    for k in range(NK):
        b_copy(k).start()
        b_copy(NK + k).start()

    lane = lax.broadcasted_iota(jnp.int32, (16, TILE), 1)
    for t in range(SLAB // TILE):
        mask[:, t * TILE:(t + 1) * TILE] = jnp.where(lane < sizes[t], 1.0, 0.0).astype(jnp.bfloat16)

    def screen(h):
        def block(i):
            for r in range(ROWS // 16):
                rows = pl.ds(r * 16, 16)
                a[h, i // 4, i % 4, rows, :] = a[h, i // 4, i % 4, rows, :] * mask[...]

        each(0, 16, block)

    def forward_half(i):
        half_copy(i).wait_recv()
        mate_copy(i, core).start()

    def settle_half(i):
        mate_copy(i, 1 - core).wait_recv()
        mate_copy(i, core).wait_send()
        half_copy(i).wait_send()

    each(1, 16, forward_half)
    each(1, 16, settle_half)
    own_copy.wait()
    screen(0)

    def copy1(h, t, j):
        part = t // NK
        there = jnp.where(part == 0, ring(0, j + 1)[0], ring(1, j + 1)[0])
        return remote(
            out1.at[h, t, j], in1.at[h, t, j], send1.at[h, t, j], recv1.at[h, t, j], (there, ao))

    def copy2(h, t, j):
        part = t // NK
        there = jnp.where(part == 0, ring(1, j + 1)[0], ring(0, j + 1)[0])
        return remote(
            out2.at[h, t, j], in2.at[h, t, j], send2.at[h, t, j], recv2.at[h, t, j], (there, ao))

    def copy3(h, t):
        return remote(
            out3.at[h, t], in3.at[1 - h, t], send3.at[h, t], recv3.at[1 - h, t], across)

    def multiply(h, k):
        for part in range(2):
            t = part * NK + k
            if h == 0:
                b_copy(t).wait()
            total[...] = jnp.dot(
                a[h].reshape(16 * ROWS, SLAB), b[:, pl.ds(pl.multiple_of(t * C, C), C)],
                preferred_element_type=jnp.float32).reshape(4, 4, ROWS, C)
            here = x if part == 0 else y

            def block_of(d):
                block = total[d] if part == 0 else total[:, d]
                return block.reshape(4 * ROWS, C)

            def push(j):
                out1[h, t, j] = encode(block_of((here + j + 1) % 4), 0)
                copy1(h, t, j).start()

            each(0, 3, push)
            own1[h, t] = block_of(here)

    def mine(t):
        return jnp.where(t // NK == 0, y, x)

    def rows_at(d):
        return pl.ds(pl.multiple_of(d * ROWS, ROWS), ROWS)

    def reduce1(h, t):
        for j in range(3):
            copy1(h, t, j).wait_recv()

        def summed(d):
            value = own1[h, t, rows_at(d), :]
            for j in range(3):
                value = value + decode(in1[h, t, j, rows_at(d), :], 0)
            return value

        def push(j):
            out2[h, t, j] = encode(summed((mine(t) + j + 1) % 4), 1)
            copy2(h, t, j).start()

        each(0, 3, push)
        own1[h, t, rows_at(mine(t)), :] = summed(mine(t))

    def reduce2(h, t):
        value = own1[h, t, rows_at(mine(t)), :]
        for j in range(3):
            copy2(h, t, j).wait_recv()
            value = value + decode(in2[h, t, j], 1)
        out3[h, t] = encode(value, 2)
        copy3(h, t).start()
        own1[h, t, rows_at(mine(t)), :] = value

    def finish(t):
        copy3(1, t).wait_recv()
        cols = pl.ds(pl.multiple_of(t * C, C), C)
        out[:, cols] = own1[0, t, rows_at(mine(t)), :] + decode(in3[0, t], 2)
        copy3(0, t).wait_recv()
        value = own1[1, t, rows_at(mine(t)), :] + decode(in3[1, t], 2)
        for l in range(C // NL):
            rows3[pl.ds(t * (C // NL) + l, ROWS, stride=LAMS), :] = value[:, l * NL:(l + 1) * NL]

    def both(k, body):
        body(k)
        body(NK + k)

    multiply(0, 0)

    each(0, 16, lambda i: z_copy(i).wait_recv())
    each(1, 16, lambda i: plane_copy(i).start())
    here_copy = pltpu.make_async_copy(
        staged.at[y * 4 + x], a.at[1, x, y, :, quarter_cols(ao)], own_sem)
    here_copy.start()

    multiply(0, 1)

    here_copy.wait()
    each(1, 16, lambda i: plane_copy(i).wait_recv())

    def relay(g):
        group_copy(0, g, ao, beside).start()
        group_copy(1, g, ao, mate).start()

    each(0, 4, relay)
    each(2, NK, lambda k: multiply(0, k))

    def relay_on(g):
        group_copy(0, g, (1 - zl) * 2 + core, beside).wait_recv()
        group_copy(2, g, (1 - zl) * 2 + core, mate).start()

    each(0, 4, relay_on)

    def settle(g):
        group_copy(1, g, zl * 2 + 1 - core, mate).wait_recv()
        group_copy(2, g, (1 - zl) * 2 + 1 - core, mate).wait_recv()
        group_copy(0, g, ao, beside).wait_send()
        group_copy(1, g, ao, mate).wait_send()
        group_copy(2, g, (1 - zl) * 2 + core, mate).wait_send()

    each(0, 4, settle)
    screen(1)

    def second(k):
        multiply(1, k)
        both(k, lambda t: reduce1(0, t))

    each(0, NK, second)

    def third(k):
        both(k, lambda t: reduce2(0, t))
        both(k, lambda t: reduce1(1, t))

    each(0, NK, third)
    each(0, NK, lambda k: both(k, lambda t: reduce2(1, t)))
    each(0, NK, lambda k: both(k, finish))

    def turn(q):
        block = rows3[pl.ds(pl.multiple_of(q * NL, NL), NL), :].T
        for d in range(4):
            out4[d, q] = block[d * LAMS:(d + 1) * LAMS]

    each(0, ROWS // 4, turn)

    def copy4(i):
        to = (ao + i) % 4
        return remote(out4.at[to], in4.at[3 - i], send4.at[i - 1], recv4.at[i - 1], (pair, to))

    for i in range(1, 4):
        copy4(i).start()
    turned[ao] = out4[ao]

    each(0, 16, lambda i: z_copy(i).wait_send())
    each(1, 16, lambda i: plane_copy(i).wait_send())

    def drain(t):
        for h in range(2):
            copy3(h, t).wait_send()
            for j in range(3):
                copy1(h, t, j).wait_send()
                copy2(h, t, j).wait_send()

    each(0, 2 * NK, drain)
    for i in range(1, 4):
        copy4(i).wait()
        turned[(ao + 4 - i) % 4] = in4[3 - i]


def ladder_rows(amps_ao, integrals, tile_sizes):
    sem = pltpu.SemaphoreType.DMA
    vmem = pltpu.VMEM
    tiles = 2 * NK
    return pl.pallas_call(
        ladder_kernel,
        out_shape=(
            jax.ShapeDtypeStruct((ROWS, COLS), jnp.float32),
            jax.ShapeDtypeStruct((4, ROWS // 4, LAMS, NL), jnp.float32),
        ),
        in_specs=[
            pl.BlockSpec(memory_space=pl.ANY),
            pl.BlockSpec(memory_space=pl.ANY),
            pl.BlockSpec(memory_space=pltpu.SMEM),
        ],
        out_specs=(pl.BlockSpec(memory_space=pltpu.VMEM), pl.BlockSpec(memory_space=pltpu.VMEM)),
        scratch_shapes=[
            vmem((2, 4, 4, ROWS, SLAB), jnp.bfloat16),
            vmem((SLAB, COLS), jnp.bfloat16),
            vmem((16, ROWS, QUARTER), jnp.bfloat16),
            vmem((4, 4, ROWS, C), jnp.float32),
            vmem((2, tiles, 4 * ROWS, C), jnp.float32),
            vmem((2, tiles, 3, 4 * ROWS, C), jnp.int16),
            vmem((2, tiles, 3, 4 * ROWS, C), jnp.int16),
            vmem((2, tiles, 3, ROWS, C), jnp.int16),
            vmem((2, tiles, 3, ROWS, C), jnp.int16),
            vmem((2, tiles, ROWS, C), jnp.int16),
            vmem((2, tiles, ROWS, C), jnp.int16),
            vmem((16, SLAB), jnp.bfloat16),
            vmem((ROWS * LAMS, NL), jnp.float32),
            vmem((4, ROWS // 4, LAMS, NL), jnp.float32),
            vmem((3, ROWS // 4, LAMS, NL), jnp.float32),
            sem((tiles,)), sem, sem((15,)), sem((15,)), sem((15,)), sem((15,)),
            sem((16,)), sem((16,)), sem((15,)), sem((15,)), sem((3, 4)), sem((3, 4)),
            sem((2, tiles, 3)), sem((2, tiles, 3)), sem((2, tiles, 3)), sem((2, tiles, 3)),
            sem((2, tiles)), sem((2, tiles)), sem((3,)), sem((3,)),
        ],
        compiler_params=pltpu.CompilerParams(
            collective_id=0, has_side_effects=True, vmem_limit_bytes=60 << 20),
        cost_estimate=pl.CostEstimate(
            flops=2 * 1024 * SLAB * COLS, bytes_accessed=24 << 20, transcendentals=0),
        name="ladder",
    )(amps_ao, integrals, tile_sizes)


def update_kernel(
    own, turned, partner, pairs, occ, vir, vir_row, amplitudes, other, residual, updated, swapped
):
    lam_first = lax.axis_index("ao") * LAMS
    lane = lax.broadcasted_iota(jnp.int32, (LAMS, NL), 1) // LAMS

    first = lax.axis_index("pair") * ROWS

    def assemble(s, carry):
        slot = lax.rem(partner[first + s], ROWS)
        q, j = lax.div(slot, 4), lax.rem(slot, 4)
        value = jnp.zeros((LAMS, NL), jnp.float32)
        for d in range(4):
            moved = pltpu.roll(turned[d, q], lax.rem(d + 4 - j, 4) * LAMS, 1)
            value = jnp.where(lane == d, moved, value)
        swapped[pl.ds(pl.multiple_of(s * LAMS, LAMS), LAMS), :] = value
        return carry

    lax.fori_loop(0, ROWS, assemble, 0, unroll=4)
    row = lax.broadcasted_iota(jnp.int32, (ROWS, NL), 0)
    occ_sum = jnp.zeros((ROWS, NL), jnp.float32)
    for s in range(ROWS):
        occ_sum = jnp.where(row == s, occ[pairs[s, 0]] + occ[pairs[s, 1]], occ_sum)
    sig = jnp.broadcast_to(vir_row[...].reshape(1, NL), (ROWS, NL))

    def finish(lam, carry):
        cols = pl.ds(pl.multiple_of(lam * NL, NL), NL)
        symmetric = 0.5 * (own[:, cols] + swapped[pl.ds(lam, ROWS, stride=LAMS), :])
        denominator = (vir[lam_first + lam] + sig) - occ_sum
        amps = amplitudes[:, cols]
        value = other[:, cols] + symmetric - denominator * amps
        residual[:, cols] = value
        updated[:, cols] = amps + value / denominator
        return carry

    lax.fori_loop(0, LAMS, finish, 0)


def update(own, turned, partner, pair_list, occ_energy, vir_energy, amplitudes, other_terms):
    smem, vmem = pl.BlockSpec(memory_space=pltpu.SMEM), pl.BlockSpec(memory_space=pltpu.VMEM)
    shape = jax.ShapeDtypeStruct((ROWS, COLS), jnp.float32)
    return pl.pallas_call(
        update_kernel,
        out_shape=(shape, shape),
        in_specs=[vmem, vmem, smem, smem, smem, smem, vmem, vmem, vmem],
        out_specs=(vmem, vmem),
        scratch_shapes=[pltpu.VMEM((ROWS * LAMS, NL), jnp.float32)],
        compiler_params=pltpu.CompilerParams(vmem_limit_bytes=32 << 20),
        cost_estimate=pl.CostEstimate(
            flops=8 * ROWS * COLS, bytes_accessed=3 << 20, transcendentals=0),
        name="update",
    )(own, turned, partner, pair_list, occ_energy, vir_energy, vir_energy, amplitudes, other_terms)


def local(
    amps_ao,
    integrals,
    tile_sizes,
    pair_list,
    partner,
    occ_energy,
    vir_energy,
    amplitudes,
    other_terms,
):
    own, turned = ladder_rows(amps_ao, integrals, tile_sizes)
    return update(own, turned, partner, pair_list, occ_energy, vir_energy, amplitudes, other_terms)


def solution(mesh):
    in_specs = (
        P("pair", None),
        P("pair", "ao"),
        P("pair"),
        P("pair", None),
        P(),
        P(),
        P(),
        P("pair", "ao"),
        P("pair", "ao"),
    )
    out_specs = (P("pair", "ao"), P("pair", "ao"))
    return jax.shard_map(local, mesh=mesh, in_specs=in_specs, out_specs=out_specs, check_vma=False)
```

```python
import functools

import jax
import jax.numpy as jnp
from jax import lax
from jax.experimental import pallas as pl
from jax.experimental.pallas import tpu as pltpu
from jax.sharding import PartitionSpec as P

NL = 128
TILE = 256
ROWS = 32
SLAB = 2048
QUARTER = SLAB // 4
COLS = 4096
LAMS = 32
C = 512
NK = COLS // 2 // C
LAGS = (1, 3, 5, 6)
MESH = pl.DeviceIdType.MESH

STEPS = 32760.0
OCTAVES = 20.17
FLOOR = 2.0**-12


def encode(value, slabs, twice=False):
    scale = jnp.where(twice, 0.5 / (FLOOR * slabs), 1.0 / (FLOOR * slabs))
    level = jnp.log2(1.0 + jnp.abs(value) * scale) * (STEPS / OCTAVES)
    level = jnp.where(value < 0.0, -level, level)
    return jnp.round(level).astype(jnp.int32).astype(jnp.int16)


def decode(code, slabs, twice=False):
    floor = jnp.where(twice, 2.0 * FLOOR * slabs, FLOOR * slabs)
    level = code.astype(jnp.int32).astype(jnp.float32)
    size = jnp.exp2(jnp.abs(level) * (OCTAVES / STEPS)) * floor - floor
    return jnp.where(level < 0.0, -size, size)


def ladder_kernel(
    amps, integrals, sizes, out, turned,
    a, b, staged, total, own1, keep, outz, inz, outo, ino, out1, in1, out2, in2, out3, in3, mask, rows3, out4, in4,
    b_sem, own_sem, here_sem, z_send, z_recv, plane_send, plane_recv, group_send, group_recv,
    sendz, recvz, sendo, recvo, send1, recv1, send2, recv2, send3, recv3, send4, recv4,
):
    pair, ao = lax.axis_index("pair"), lax.axis_index("ao")
    zh, y, x = pair // 16, (pair // 4) % 4, pair % 4
    zl, core = ao // 2, ao % 2
    mate = (pair, zl * 2 + 1 - core)
    beside = (pair, (1 - zl) * 2 + core)
    opposite = ((1 - zh) * 16 + y * 4 + x, (1 - zl) * 2 + core)
    across = ((1 - zh) * 16 + y * 4 + x, ao)

    def in_plane(i):
        return ((y + i // 4) % 4) * 4 + (x + i % 4) % 4

    def ring(part, j):
        if part == 0:
            return zh * 16 + y * 4 + (x + j) % 4, ao
        return zh * 16 + ((y + j) % 4) * 4 + x, ao

    def remote(src, dst, send, recv, device):
        return pltpu.make_async_remote_copy(
            src_ref=src, dst_ref=dst, send_sem=send, recv_sem=recv,
            device_id=device, device_id_type=MESH)

    def sent(ref, sem):
        remote(ref, ref, sem, sem, mate).wait_send()

    def received(ref, sem):
        remote(ref, ref, sem, sem, mate).wait_recv()

    def each(first, last, body):
        def step(i, carry):
            body(i)
            return carry

        lax.fori_loop(first, last, step, 0)

    barrier = pltpu.get_barrier_semaphore()

    def greet(peer):
        pl.semaphore_signal(barrier, inc=1, device_id=peer, device_id_type=MESH)

    each(1, 16, lambda i: greet((zh * 16 + in_plane(i), ao)))
    for peer in (opposite, across, *((pair, (ao + i) % 4) for i in range(1, 4))):
        greet(peer)
    pl.semaphore_wait(barrier, 20)

    def quarter_cols(quarter):
        return pl.ds(pl.multiple_of(quarter * QUARTER, QUARTER), QUARTER)

    def amp_cols(position, quarter):
        return amps.at[:, pl.ds(pl.multiple_of(position * SLAB + quarter * QUARTER, QUARTER), QUARTER)]

    def z_copy(i):
        return remote(
            amp_cols((1 - zh) * 16 + i, (1 - zl) * 2 + core), staged.at[i],
            z_send, z_recv, opposite)

    def plane_copy(h, i):
        there = in_plane(i)
        return remote(
            amp_cols(zh * 16 + there, ao) if h == 0 else staged.at[there],
            a.at[h, x, y, :, quarter_cols(ao)],
            plane_send.at[h], plane_recv.at[h, i % 4], (zh * 16 + there, ao))

    def group_copy(h, kind, g, quarter, device):
        block = a.at[h, (x + 4 - g) % 4, :, :, quarter_cols(quarter)]
        recv = group_recv.at[h, g if kind == 0 else 3 + kind]
        return remote(block, block, group_send.at[h], recv, device)

    def relay(h, g):
        column = a.at[h, (x + 4 - g) % 4, :, :, quarter_cols(ao)]
        received(column if g else column.at[pl.ds(0, 3)], plane_recv.at[h, g])
        group_copy(h, 0, g, ao, beside).start()
        group_copy(h, 1, g, ao, mate).start()

    def relay_on(h, g):
        group_copy(h, 0, g, (1 - zl) * 2 + core, beside).wait_recv()
        group_copy(h, 2, g, (1 - zl) * 2 + core, mate).start()

    def settle(h):
        whole = a.at[h, :, :, :, quarter_cols(0)]
        received(whole, group_recv.at[h, 4])
        received(whole, group_recv.at[h, 5])
        sent(a.at[h, :, :, :, pl.ds(0, 3 * QUARTER)], group_send.at[h])

    each(1, 16, lambda i: plane_copy(0, (i % 4) * 4 + i // 4).start())
    each(0, 16, lambda i: z_copy(i).start())
    own_copy = pltpu.make_async_copy(
        amp_cols(pair, ao), a.at[0, x, y, :, quarter_cols(ao)], own_sem)
    own_copy.start()

    def b_copy(t):
        cols = pl.ds(t * C, C)
        return pltpu.make_async_copy(integrals.at[:, cols], b.at[:, cols], b_sem.at[t])

    for k in range(NK):
        b_copy(k).start()
        b_copy(NK + k).start()

    lane = lax.broadcasted_iota(jnp.int32, (16, TILE), 1)
    for t in range(SLAB // TILE):
        mask[:, t * TILE:(t + 1) * TILE] = jnp.where(lane < sizes[t], 1.0, 0.0).astype(jnp.bfloat16)

    def screen(h):
        def block(i):
            for r in range(ROWS // 16):
                rows = pl.ds(r * 16, 16)
                a[h, i // 4, i % 4, rows, :] = a[h, i // 4, i % 4, rows, :] * mask[...]

        each(0, 16, block)

    own_copy.wait()
    for g in range(4):
        relay(0, g)
    for g in range(4):
        relay_on(0, g)
    received(staged, z_recv)
    each(1, 16, lambda i: plane_copy(1, (i % 4) * 4 + i // 4).start())
    here_copy = pltpu.make_async_copy(
        staged.at[y * 4 + x], a.at[1, x, y, :, quarter_cols(ao)], here_sem)
    here_copy.start()
    settle(0)
    screen(0)

    def neighbour(t, side):
        along_x, along_y = ring(0, 1 + 2 * side)[0], ring(1, 1 + 2 * side)[0]
        return jnp.where(t // NK == 0, along_x, along_y), ao

    LAST = NK - 1

    def slot(h, t):
        return jnp.where(h == 0, t // NK * LAST + t % NK, 2 * LAST + t)

    def pair_slot(h, k):
        return jnp.where(h == 0, k, LAST + k)

    def copyo(s, t, side):
        return remote(
            outo.at[s, side], ino.at[s, side], sendo, recvo.at[s], neighbour(t, side))

    def copy1(s, t, side):
        return remote(
            out1.at[s, side], in1.at[s, side], send1, recv1.at[s], neighbour(t, side))

    def copy2(s, t, j):
        part = t // NK
        there = jnp.where(part == 0, ring(1, j + 1)[0], ring(0, j + 1)[0])
        return remote(out2.at[s, j], in2.at[s, j], send2, recv2.at[s], (there, ao))

    def copy3(h, k):
        to = (1 - h) * NK + k
        return remote(out3.at[pair_slot(h, k)], in3.at[to], send3, recv3.at[to], across)

    def copyz(part):
        return remote(outz.at[part], inz.at[part], sendz, recvz.at[part], across)

    def multiply(n):
        h, k = n // NK, n % NK
        for part in range(2):
            t = part * NK + k

            @pl.when(h == 0)
            def _():
                b_copy(t).wait()

            total[...] = jnp.dot(
                a[h].reshape(16 * ROWS, SLAB), b[:, pl.ds(pl.multiple_of(t * C, C), C)],
                preferred_element_type=jnp.float32).reshape(4, 4, ROWS, C)
            here = x if part == 0 else y

            @pl.when(n == LAST)
            def _():
                def block(d):
                    outz[part, d] = encode(total[d], 1)

                each(0, 4, block)
                copyz(part).start()

            @pl.when(n == NK + LAST)
            def _():
                copyz(part).wait_recv()

                def block(d):
                    total[d] = total[d] + decode(inz[part, d], 1)

                each(0, 4, block)

            def block_of(d):
                block = total[d] if part == 0 else total[:, d]
                return block.reshape(4 * ROWS, C)

            @pl.when(n != LAST)
            def _():
                across_block = block_of((here + 2) % 4)
                s = slot(h, t)
                for side in range(2):
                    outo[s, side] = encode(
                        across_block[:, side * C // 2:(side + 1) * C // 2], 1, k == LAST)
                    copyo(s, t, side).start()
                for side in range(2):
                    keep[t, side] = block_of((here + 1 + 2 * side) % 4)
                own1[h, t] = block_of(here)

    def combine(h, t):
        s, twice = slot(h, t), t % NK == LAST
        received(ino.at[s], recvo.at[s])
        for side in range(2):
            half = slice(side * C // 2, (side + 1) * C // 2)
            rest = slice((1 - side) * C // 2, (2 - side) * C // 2)
            out1[s, side, :, half] = encode(
                keep[t, side, :, half] + decode(ino[s, side], 1, twice), 2, twice)
            out1[s, side, :, rest] = encode(keep[t, side, :, rest], 2, twice)
            copy1(s, t, side).start()

    def mine(t):
        return jnp.where(t // NK == 0, y, x)

    def rows_at(d):
        return pl.ds(pl.multiple_of(d * ROWS, ROWS), ROWS)

    def reduce1(h, t):
        s, twice = slot(h, t), t % NK == LAST
        received(in1.at[s], recv1.at[s])

        def summed(d):
            value = own1[h, t, rows_at(d), :]
            for side in range(2):
                value = value + decode(in1[s, side, rows_at(d), :], 2, twice)
            return value

        def push(j):
            out2[s, j] = encode(summed((mine(t) + j + 1) % 4), 4, twice)
            copy2(s, t, j).start()

        each(0, 3, push)
        own1[h, t, rows_at(mine(t)), :] = summed(mine(t))

    def reduce2(h, k):
        twice = k == LAST
        for part in range(2):
            t = part * NK + k
            s = slot(h, t)
            received(in2.at[s], recv2.at[s])
            value = own1[h, t, rows_at(mine(t)), :]
            for j in range(3):
                value = value + decode(in2[s, j], 4, twice)
            out3[pair_slot(h, k), part] = encode(value, 16, twice)
            own1[h, t, rows_at(mine(t)), :] = value
        copy3(h, k).start()

    def finish(k, last):
        received(in3.at[k], recv3.at[k])
        if not last:
            received(in3.at[NK + k], recv3.at[NK + k])
        for part in range(2):
            t = part * NK + k
            cols = pl.ds(pl.multiple_of(t * C, C), C)
            value = own1[1, t, rows_at(mine(t)), :]
            if last:
                out[:, cols] = decode(in3[k, part], 32)
            else:
                out[:, cols] = own1[0, t, rows_at(mine(t)), :] + decode(in3[k, part], 16)
                value = value + decode(in3[NK + k, part], 16)
            for l in range(C // NL):
                rows3[pl.ds(t * (C // NL) + l, ROWS, stride=LAMS), :] = (
                    value[:, l * NL:(l + 1) * NL])

    def both(k, body):
        body(k)
        body(NK + k)

    def step(n):
        def at(lag, body):
            @pl.when((n >= lag) & (n < lag + 2 * NK) & (n != lag + LAST))
            def _():
                body((n - lag) // NK, (n - lag) % NK)

        def tiles_at(lag, body):
            at(lag, lambda h, k: both(k, lambda t: body(h, t)))

        @pl.when((n < 2 * NK) & (n != NK))
        def _():
            multiply(n)

        @pl.when(n == 0)
        def _():
            here_copy.wait()
            for g in range(4):
                relay(1, g)

        tiles_at(LAGS[0], combine)
        tiles_at(LAGS[1], reduce1)
        at(LAGS[2], reduce2)

        @pl.when((n >= NK + LAGS[3]) & (n < NK + LAGS[3] + LAST))
        def _():
            finish(n - NK - LAGS[3], False)

        @pl.when(n == NK)
        def _():
            for g in range(4):
                relay_on(1, g)
            settle(1)
            screen(1)
            multiply(n)

    each(0, NK + max(LAGS[3] + LAST, LAGS[2] + NK), step)
    finish(LAST, True)

    def turn(q):
        block = rows3[pl.ds(pl.multiple_of(q * NL, NL), NL), :].T
        for d in range(4):
            out4[d, q] = encode(block[d * LAMS:(d + 1) * LAMS], 32)

    each(0, ROWS // 4, turn)

    def copy4(i):
        to = (ao + i) % 4
        return remote(out4.at[to], in4.at[3 - i], send4, recv4, (pair, to))

    for i in range(1, 4):
        copy4(i).start()
    turned[ao] = out4[ao]

    sent(staged, z_send)
    for h in range(2):
        sent(staged.at[pl.ds(0, 15)], plane_send.at[h])
    for ref, sem in (
        (outo, sendo), (out1, send1), (out2, send2), (out3, send3), (outz, sendz),
        (out4.at[pl.ds(0, 3)], send4),
    ):
        sent(ref, sem)
    received(in4, recv4)
    for i in range(1, 4):
        turned[(ao + 4 - i) % 4] = in4[3 - i]


def ladder_rows(amps_ao, integrals, tile_sizes):
    sem = pltpu.SemaphoreType.DMA
    vmem = pltpu.VMEM
    tiles, slots = 2 * NK, 4 * NK - 2
    return pl.pallas_call(
        ladder_kernel,
        out_shape=(
            jax.ShapeDtypeStruct((ROWS, COLS), jnp.float32),
            jax.ShapeDtypeStruct((4, ROWS // 4, LAMS, NL), jnp.int16),
        ),
        in_specs=[
            pl.BlockSpec(memory_space=pl.ANY),
            pl.BlockSpec(memory_space=pl.ANY),
            pl.BlockSpec(memory_space=pltpu.SMEM),
        ],
        out_specs=(pl.BlockSpec(memory_space=pltpu.VMEM), pl.BlockSpec(memory_space=pltpu.VMEM)),
        scratch_shapes=[
            vmem((2, 4, 4, ROWS, SLAB), jnp.bfloat16),
            vmem((SLAB, COLS), jnp.bfloat16),
            vmem((16, ROWS, QUARTER), jnp.bfloat16),
            vmem((4, 4, ROWS, C), jnp.float32),
            vmem((2, tiles, 4 * ROWS, C), jnp.float32),
            vmem((tiles, 2, 4 * ROWS, C), jnp.float32),
            vmem((2, 4, 4, ROWS, C), jnp.int16),
            vmem((2, 4, 4, ROWS, C), jnp.int16),
            vmem((slots, 2, 4 * ROWS, C // 2), jnp.int16),
            vmem((slots, 2, 4 * ROWS, C // 2), jnp.int16),
            vmem((slots, 2, 4 * ROWS, C), jnp.int16),
            vmem((slots, 2, 4 * ROWS, C), jnp.int16),
            vmem((slots, 3, ROWS, C), jnp.int16),
            vmem((slots, 3, ROWS, C), jnp.int16),
            vmem((slots // 2, 2, ROWS, C), jnp.int16),
            vmem((tiles, 2, ROWS, C), jnp.int16),
            vmem((16, SLAB), jnp.bfloat16),
            vmem((ROWS * LAMS, NL), jnp.float32),
            vmem((4, ROWS // 4, LAMS, NL), jnp.int16),
            vmem((3, ROWS // 4, LAMS, NL), jnp.int16),
            sem((tiles,)), sem, sem, sem, sem, sem((2,)), sem((2, 4)), sem((2,)), sem((2, 6)),
            sem, sem((2,)), sem, sem((slots,)), sem, sem((slots,)), sem, sem((slots,)),
            sem, sem((tiles,)), sem, sem,
        ],
        compiler_params=pltpu.CompilerParams(
            collective_id=0, has_side_effects=True, vmem_limit_bytes=60 << 20),
        cost_estimate=pl.CostEstimate(
            flops=2 * 1024 * SLAB * COLS, bytes_accessed=24 << 20, transcendentals=0),
        name="ladder",
    )(amps_ao, integrals, tile_sizes)


def update_kernel(
    own_hbm, turned_hbm, partner, pairs, occ, vir, vir_row, amplitudes_hbm, other_hbm,
    residual, updated, swapped, own, turned, amplitudes, other, sem
):
    turned_copy = pltpu.make_async_copy(turned_hbm, turned, sem.at[0])
    row_copies = [
        pltpu.make_async_copy(src, dst, sem.at[i + 1])
        for i, (src, dst) in enumerate(
            ((own_hbm, own), (amplitudes_hbm, amplitudes), (other_hbm, other)))]
    turned_copy.start()
    for copy in row_copies:
        copy.start()
    lam_first = lax.axis_index("ao") * LAMS
    lane = lax.broadcasted_iota(jnp.int32, (LAMS, NL), 1) // LAMS

    row = lax.broadcasted_iota(jnp.int32, (ROWS, NL), 0)
    occ_sum = jnp.zeros((ROWS, NL), jnp.float32)
    for s in range(ROWS):
        occ_sum = jnp.where(row == s, occ[pairs[0, s]] + occ[pairs[1, s]], occ_sum)
    sig = jnp.broadcast_to(vir_row[...].reshape(1, NL), (ROWS, NL))

    turned_copy.wait()
    first = lax.axis_index("pair") * ROWS

    def assemble(s, carry):
        slot = lax.rem(partner[first + s], ROWS)
        q, j = lax.div(slot, 4), lax.rem(slot, 4)
        value = jnp.zeros((LAMS, NL), jnp.float32)
        for d in range(4):
            moved = pltpu.roll(decode(turned[d, q], 32), lax.rem(d + 4 - j, 4) * LAMS, 1)
            value = jnp.where(lane == d, moved, value)
        swapped[pl.ds(pl.multiple_of(s * LAMS, LAMS), LAMS), :] = value
        return carry

    lax.fori_loop(0, ROWS, assemble, 0, unroll=4)
    for copy in row_copies:
        copy.wait()

    def finish(lam, carry):
        cols = pl.ds(pl.multiple_of(lam * NL, NL), NL)
        symmetric = 0.5 * (own[:, cols] + swapped[pl.ds(lam, ROWS, stride=LAMS), :])
        denominator = (vir[lam_first + lam] + sig) - occ_sum
        amps = amplitudes[:, cols]
        value = other[:, cols] + symmetric - denominator * amps
        residual[:, cols] = value
        updated[:, cols] = amps + value / denominator
        return carry

    lax.fori_loop(0, LAMS, finish, 0)


def update(own, turned, partner, pair_list, occ_energy, vir_energy, amplitudes, other_terms):
    hbm = pl.BlockSpec(memory_space=pl.ANY)
    smem, vmem = pl.BlockSpec(memory_space=pltpu.SMEM), pl.BlockSpec(memory_space=pltpu.VMEM)
    shape = jax.ShapeDtypeStruct((ROWS, COLS), jnp.float32)
    return pl.pallas_call(
        update_kernel,
        out_shape=(shape, shape),
        in_specs=[hbm, hbm, smem, smem, smem, smem, vmem, hbm, hbm],
        out_specs=(vmem, vmem),
        scratch_shapes=[
            pltpu.VMEM((ROWS * LAMS, NL), jnp.float32),
            pltpu.VMEM((ROWS, COLS), jnp.float32),
            pltpu.VMEM((4, ROWS // 4, LAMS, NL), jnp.int16),
            pltpu.VMEM((ROWS, COLS), jnp.float32),
            pltpu.VMEM((ROWS, COLS), jnp.float32),
            pltpu.SemaphoreType.DMA((4,)),
        ],
        compiler_params=pltpu.CompilerParams(vmem_limit_bytes=60 << 20),
        cost_estimate=pl.CostEstimate(
            flops=8 * ROWS * COLS, bytes_accessed=3 << 20, transcendentals=0),
        name="update",
    )(own, turned, partner, pair_list.T, occ_energy, vir_energy, vir_energy, amplitudes, other_terms)


def local(
    amps_ao,
    integrals,
    tile_sizes,
    pair_list,
    partner,
    occ_energy,
    vir_energy,
    amplitudes,
    other_terms,
):
    own, turned = ladder_rows(amps_ao, integrals, tile_sizes)
    return update(own, turned, partner, pair_list, occ_energy, vir_energy, amplitudes, other_terms)


def solution(mesh):
    in_specs = (
        P("pair", None),
        P("pair", "ao"),
        P("pair"),
        P("pair", None),
        P(),
        P(),
        P(),
        P("pair", "ao"),
        P("pair", "ao"),
    )
    out_specs = (P("pair", "ao"), P("pair", "ao"))
    return jax.shard_map(local, mesh=mesh, in_specs=in_specs, out_specs=out_specs, check_vma=False)
```

```python
import functools

import jax
import jax.numpy as jnp
from jax import lax
from jax.experimental import pallas as pl
from jax.experimental.pallas import tpu as pltpu
from jax.sharding import PartitionSpec as P

NL = 128
TILE = 256
ROWS = 32
SLAB = 2048
QUARTER = SLAB // 4
COLS = 4096
LAMS = 32
C = 512
NK = COLS // 2 // C
LAGS = (1, 3, 5, 6)
MESH = pl.DeviceIdType.MESH

STEPS = 32760.0
OCTAVES = 20.17
FLOOR = 2.0**-12


def encode(value, slabs, twice=False):
    scale = jnp.where(twice, 0.5 / (FLOOR * slabs), 1.0 / (FLOOR * slabs))
    level = jnp.log2(1.0 + jnp.abs(value) * scale) * (STEPS / OCTAVES)
    level = jnp.where(value < 0.0, -level, level)
    return jnp.round(level).astype(jnp.int32).astype(jnp.int16)


def decode(code, slabs, twice=False):
    floor = jnp.where(twice, 2.0 * FLOOR * slabs, FLOOR * slabs)
    level = code.astype(jnp.int32).astype(jnp.float32)
    size = jnp.exp2(jnp.abs(level) * (OCTAVES / STEPS)) * floor - floor
    return jnp.where(level < 0.0, -size, size)


def ladder_kernel(
    amps, integrals, sizes, out, turned,
    a, b, staged, near, total, own1, keep, outz, inz, outo, ino, out1, in1, out2, in2, out3, in3, mask, rows3, out4, in4,
    b_sem, own_sem, here_sem, z_send, z_recv, plane_send, plane_recv, group_send, group_recv,
    sendz, recvz, sendo, recvo, send1, recv1, send2, recv2, send3, recv3, send4, recv4,
):
    pair, ao = lax.axis_index("pair"), lax.axis_index("ao")
    zh, y, x = pair // 16, (pair // 4) % 4, pair % 4
    zl, core = ao // 2, ao % 2
    mate = (pair, zl * 2 + 1 - core)
    beside = (pair, (1 - zl) * 2 + core)
    opposite = ((1 - zh) * 16 + y * 4 + x, (1 - zl) * 2 + core)
    across = ((1 - zh) * 16 + y * 4 + x, ao)

    def in_plane(i):
        return ((y + i // 4) % 4) * 4 + (x + i % 4) % 4

    def ring(part, j):
        if part == 0:
            return zh * 16 + y * 4 + (x + j) % 4, ao
        return zh * 16 + ((y + j) % 4) * 4 + x, ao

    def remote(src, dst, send, recv, device):
        return pltpu.make_async_remote_copy(
            src_ref=src, dst_ref=dst, send_sem=send, recv_sem=recv,
            device_id=device, device_id_type=MESH)

    def sent(ref, sem):
        remote(ref, ref, sem, sem, mate).wait_send()

    def received(ref, sem):
        remote(ref, ref, sem, sem, mate).wait_recv()

    def each(first, last, body):
        def step(i, carry):
            body(i)
            return carry

        lax.fori_loop(first, last, step, 0)

    barrier = pltpu.get_barrier_semaphore()

    def greet(peer):
        pl.semaphore_signal(barrier, inc=1, device_id=peer, device_id_type=MESH)

    each(1, 16, lambda i: greet((zh * 16 + in_plane(i), ao)))
    for peer in (opposite, across, *((pair, (ao + i) % 4) for i in range(1, 4))):
        greet(peer)
    pl.semaphore_wait(barrier, 20)

    def quarter_cols(quarter):
        return pl.ds(pl.multiple_of(quarter * QUARTER, QUARTER), QUARTER)

    def amp_cols(position, quarter):
        return amps.at[:, pl.ds(pl.multiple_of(position * SLAB + quarter * QUARTER, QUARTER), QUARTER)]

    def z_copy(i):
        return remote(
            amp_cols((1 - zh) * 16 + i, (1 - zl) * 2 + core), staged.at[i],
            z_send, z_recv, opposite)

    def plane_copy(h, i):
        there = in_plane(i)
        return remote(
            amp_cols(zh * 16 + there, ao) if h == 0 else staged.at[there],
            a.at[h, x, y, :, quarter_cols(ao)],
            plane_send.at[h], plane_recv.at[h, i % 4], (zh * 16 + there, ao))

    def group_copy(h, kind, g, quarter, device):
        block = a.at[h, (x + 4 - g) % 4, :, :, quarter_cols(quarter)]
        recv = group_recv.at[h, g if kind == 0 else 3 + kind]
        return remote(block, block, group_send.at[h], recv, device)

    def relay(h, g):
        column = a.at[h, (x + 4 - g) % 4, :, :, quarter_cols(ao)]
        received(column if g else column.at[pl.ds(0, 3)], plane_recv.at[h, g])

        def screen(i):
            rows = pl.ds(pl.multiple_of(i % 2 * 16, 16), 16)
            column[i // 2, rows, :] = column[i // 2, rows, :] * mask[:, quarter_cols(ao)]

        each(0, 2 * 4, screen)
        group_copy(h, 0, g, ao, beside).start()
        group_copy(h, 1, g, ao, mate).start()

    def relay_on(h, g):
        group_copy(h, 0, g, (1 - zl) * 2 + core, beside).wait_recv()
        group_copy(h, 2, g, (1 - zl) * 2 + core, mate).start()

    def relayed(h, kind):
        received(a.at[h, :, :, :, quarter_cols(0)], group_recv.at[h, 3 + kind])

    each(1, 16, lambda i: plane_copy(0, (i % 4) * 4 + i // 4).start())
    each(0, 16, lambda i: z_copy(i).start())
    own_copy = pltpu.make_async_copy(
        amp_cols(pair, ao), a.at[0, x, y, :, quarter_cols(ao)], own_sem)
    own_copy.start()

    def b_copy(t):
        cols = pl.ds(t * C, C)
        return pltpu.make_async_copy(integrals.at[:, cols], b.at[:, cols], b_sem.at[t])

    for k in range(NK):
        b_copy(k).start()
        b_copy(NK + k).start()

    lane = lax.broadcasted_iota(jnp.int32, (16, TILE), 1)
    for t in range(SLAB // TILE):
        mask[:, t * TILE:(t + 1) * TILE] = jnp.where(lane < sizes[t], 1.0, 0.0).astype(jnp.bfloat16)

    own_copy.wait()
    for g in range(4):
        relay(0, g)
    relayed(0, 1)

    def k_half(side):
        return pl.ds(pl.multiple_of(side * SLAB // 2, SLAB // 2), SLAB // 2)

    def half_product(h, t, side):
        return jnp.dot(
            a[h, :, :, :, k_half(side)].reshape(16 * ROWS, SLAB // 2),
            b[k_half(side), pl.ds(pl.multiple_of(t * C, C), C)],
            preferred_element_type=jnp.float32)

    def early(h, g):
        for t in (g, NK + g):
            if h == 0:
                b_copy(t).wait()
            near[t] = half_product(h, t, zl)
        relay_on(h, g)

    each(0, NK - 1, lambda g: early(0, g))
    received(staged, z_recv)
    each(1, 16, lambda i: plane_copy(1, (i % 4) * 4 + i // 4).start())
    here_copy = pltpu.make_async_copy(
        staged.at[y * 4 + x], a.at[1, x, y, :, quarter_cols(ao)], here_sem)
    here_copy.start()
    early(0, NK - 1)
    relayed(0, 2)

    def neighbour(t, side):
        along_x, along_y = ring(0, 1 + 2 * side)[0], ring(1, 1 + 2 * side)[0]
        return jnp.where(t // NK == 0, along_x, along_y), ao

    LAST = NK - 1

    def slot(h, t):
        return jnp.where(h == 0, t // NK * LAST + t % NK, 2 * LAST + t)

    def pair_slot(h, k):
        return jnp.where(h == 0, k, LAST + k)

    def copyo(s, t, side):
        return remote(
            outo.at[s, side], ino.at[s, side], sendo, recvo.at[s], neighbour(t, side))

    def copy1(s, t, side):
        return remote(
            out1.at[s, side], in1.at[s, side], send1, recv1.at[s], neighbour(t, side))

    def copy2(s, t, j):
        part = t // NK
        there = jnp.where(part == 0, ring(1, j + 1)[0], ring(0, j + 1)[0])
        return remote(out2.at[s, j], in2.at[s, j], send2, recv2.at[s], (there, ao))

    def copy3(h, k):
        to = (1 - h) * NK + k
        return remote(out3.at[pair_slot(h, k)], in3.at[to], send3, recv3.at[to], across)

    def copyz(part):
        return remote(outz.at[part], inz.at[part], sendz, recvz.at[part], across)

    def multiply(n):
        h, k = n // NK, n % NK
        for part in range(2):
            t = part * NK + k

            total[...] = (near[t] + half_product(h, t, 1 - zl)).reshape(4, 4, ROWS, C)
            here = x if part == 0 else y

            @pl.when(n == LAST)
            def _():
                def block(d):
                    outz[part, d] = encode(total[d], 1)

                each(0, 4, block)
                copyz(part).start()

            @pl.when(n == NK + LAST)
            def _():
                copyz(part).wait_recv()

                def block(d):
                    total[d] = total[d] + decode(inz[part, d], 1)

                each(0, 4, block)

            def block_of(d):
                block = total[d] if part == 0 else total[:, d]
                return block.reshape(4 * ROWS, C)

            @pl.when(n != LAST)
            def _():
                across_block = block_of((here + 2) % 4)
                s = slot(h, t)
                for side in range(2):
                    outo[s, side] = encode(
                        across_block[:, side * C // 2:(side + 1) * C // 2], 1, k == LAST)
                    copyo(s, t, side).start()
                for side in range(2):
                    keep[t, side] = block_of((here + 1 + 2 * side) % 4)
                own1[h, t] = block_of(here)

    def combine(h, t):
        s, twice = slot(h, t), t % NK == LAST
        received(ino.at[s], recvo.at[s])
        for side in range(2):
            half = slice(side * C // 2, (side + 1) * C // 2)
            rest = slice((1 - side) * C // 2, (2 - side) * C // 2)
            out1[s, side, :, half] = encode(
                keep[t, side, :, half] + decode(ino[s, side], 1, twice), 2, twice)
            out1[s, side, :, rest] = encode(keep[t, side, :, rest], 2, twice)
            copy1(s, t, side).start()

    def mine(t):
        return jnp.where(t // NK == 0, y, x)

    def rows_at(d):
        return pl.ds(pl.multiple_of(d * ROWS, ROWS), ROWS)

    def reduce1(h, t):
        s, twice = slot(h, t), t % NK == LAST
        received(in1.at[s], recv1.at[s])

        def summed(d):
            value = own1[h, t, rows_at(d), :]
            for side in range(2):
                value = value + decode(in1[s, side, rows_at(d), :], 2, twice)
            return value

        def push(j):
            out2[s, j] = encode(summed((mine(t) + j + 1) % 4), 4, twice)
            copy2(s, t, j).start()

        each(0, 3, push)
        own1[h, t, rows_at(mine(t)), :] = summed(mine(t))

    def reduce2(h, k):
        twice = k == LAST
        for part in range(2):
            t = part * NK + k
            s = slot(h, t)
            received(in2.at[s], recv2.at[s])
            value = own1[h, t, rows_at(mine(t)), :]
            for j in range(3):
                value = value + decode(in2[s, j], 4, twice)
            out3[pair_slot(h, k), part] = encode(value, 16, twice)
            own1[h, t, rows_at(mine(t)), :] = value
        copy3(h, k).start()

    def finish(k, last):
        received(in3.at[k], recv3.at[k])
        if not last:
            received(in3.at[NK + k], recv3.at[NK + k])
        for part in range(2):
            t = part * NK + k
            cols = pl.ds(pl.multiple_of(t * C, C), C)
            value = own1[1, t, rows_at(mine(t)), :]
            if last:
                out[:, cols] = decode(in3[k, part], 32)
            else:
                out[:, cols] = own1[0, t, rows_at(mine(t)), :] + decode(in3[k, part], 16)
                value = value + decode(in3[NK + k, part], 16)
            for l in range(C // NL):
                rows3[pl.ds(t * (C // NL) + l, ROWS, stride=LAMS), :] = (
                    value[:, l * NL:(l + 1) * NL])

    def both(k, body):
        body(k)
        body(NK + k)

    def step(n):
        def at(lag, body):
            @pl.when((n >= lag) & (n < lag + 2 * NK) & (n != lag + LAST))
            def _():
                body((n - lag) // NK, (n - lag) % NK)

        def tiles_at(lag, body):
            at(lag, lambda h, k: both(k, lambda t: body(h, t)))

        @pl.when((n < 2 * NK) & (n != NK))
        def _():
            multiply(n)

        @pl.when(n == 0)
        def _():
            here_copy.wait()
            for g in range(4):
                relay(1, g)

        tiles_at(LAGS[0], combine)
        tiles_at(LAGS[1], reduce1)
        at(LAGS[2], reduce2)

        @pl.when((n >= NK + LAGS[3]) & (n < NK + LAGS[3] + LAST))
        def _():
            finish(n - NK - LAGS[3], False)

        @pl.when(n == NK)
        def _():
            relayed(1, 1)
            each(0, NK, lambda g: early(1, g))
            relayed(1, 2)
            multiply(n)

    each(0, NK + max(LAGS[3] + LAST, LAGS[2] + NK), step)
    finish(LAST, True)

    def turn(q):
        block = rows3[pl.ds(pl.multiple_of(q * NL, NL), NL), :].T
        for d in range(4):
            out4[d, q] = encode(block[d * LAMS:(d + 1) * LAMS], 32)

    each(0, ROWS // 4, turn)

    def copy4(i):
        to = (ao + i) % 4
        return remote(out4.at[to], in4.at[3 - i], send4, recv4, (pair, to))

    for i in range(1, 4):
        copy4(i).start()
    turned[ao] = out4[ao]

    sent(staged, z_send)
    for h in range(2):
        sent(staged.at[pl.ds(0, 15)], plane_send.at[h])
        sent(a.at[h, :, :, :, pl.ds(0, 3 * QUARTER)], group_send.at[h])
    for ref, sem in (
        (outo, sendo), (out1, send1), (out2, send2), (out3, send3), (outz, sendz),
        (out4.at[pl.ds(0, 3)], send4),
    ):
        sent(ref, sem)
    received(in4, recv4)
    for i in range(1, 4):
        turned[(ao + 4 - i) % 4] = in4[3 - i]


def ladder_rows(amps_ao, integrals, tile_sizes):
    sem = pltpu.SemaphoreType.DMA
    vmem = pltpu.VMEM
    tiles, slots = 2 * NK, 4 * NK - 2
    return pl.pallas_call(
        ladder_kernel,
        out_shape=(
            jax.ShapeDtypeStruct((ROWS, COLS), jnp.float32),
            jax.ShapeDtypeStruct((4, ROWS // 4, LAMS, NL), jnp.int16),
        ),
        in_specs=[
            pl.BlockSpec(memory_space=pl.ANY),
            pl.BlockSpec(memory_space=pl.ANY),
            pl.BlockSpec(memory_space=pltpu.SMEM),
        ],
        out_specs=(pl.BlockSpec(memory_space=pltpu.VMEM), pl.BlockSpec(memory_space=pltpu.VMEM)),
        scratch_shapes=[
            vmem((2, 4, 4, ROWS, SLAB), jnp.bfloat16),
            vmem((SLAB, COLS), jnp.bfloat16),
            vmem((16, ROWS, QUARTER), jnp.bfloat16),
            vmem((tiles, 16 * ROWS, C), jnp.float32),
            vmem((4, 4, ROWS, C), jnp.float32),
            vmem((2, tiles, 4 * ROWS, C), jnp.float32),
            vmem((tiles, 2, 4 * ROWS, C), jnp.float32),
            vmem((2, 4, 4, ROWS, C), jnp.int16),
            vmem((2, 4, 4, ROWS, C), jnp.int16),
            vmem((slots, 2, 4 * ROWS, C // 2), jnp.int16),
            vmem((slots, 2, 4 * ROWS, C // 2), jnp.int16),
            vmem((slots, 2, 4 * ROWS, C), jnp.int16),
            vmem((slots, 2, 4 * ROWS, C), jnp.int16),
            vmem((slots, 3, ROWS, C), jnp.int16),
            vmem((slots, 3, ROWS, C), jnp.int16),
            vmem((slots // 2, 2, ROWS, C), jnp.int16),
            vmem((tiles, 2, ROWS, C), jnp.int16),
            vmem((16, SLAB), jnp.bfloat16),
            vmem((ROWS * LAMS, NL), jnp.float32),
            vmem((4, ROWS // 4, LAMS, NL), jnp.int16),
            vmem((3, ROWS // 4, LAMS, NL), jnp.int16),
            sem((tiles,)), sem, sem, sem, sem, sem((2,)), sem((2, 4)), sem((2,)), sem((2, 6)),
            sem, sem((2,)), sem, sem((slots,)), sem, sem((slots,)), sem, sem((slots,)),
            sem, sem((tiles,)), sem, sem,
        ],
        compiler_params=pltpu.CompilerParams(
            collective_id=0, has_side_effects=True, vmem_limit_bytes=60 << 20),
        cost_estimate=pl.CostEstimate(
            flops=2 * 1024 * SLAB * COLS, bytes_accessed=24 << 20, transcendentals=0),
        name="ladder",
    )(amps_ao, integrals, tile_sizes)


def update_kernel(
    own_hbm, turned_hbm, partner, pairs, occ, vir, vir_row, amplitudes_hbm, other_hbm,
    residual, updated, swapped, own, turned, amplitudes, other, sem
):
    turned_copy = pltpu.make_async_copy(turned_hbm, turned, sem.at[0])
    row_copies = [
        pltpu.make_async_copy(src, dst, sem.at[i + 1])
        for i, (src, dst) in enumerate(
            ((own_hbm, own), (amplitudes_hbm, amplitudes), (other_hbm, other)))]
    turned_copy.start()
    for copy in row_copies:
        copy.start()
    lam_first = lax.axis_index("ao") * LAMS
    lane = lax.broadcasted_iota(jnp.int32, (LAMS, NL), 1) // LAMS

    row = lax.broadcasted_iota(jnp.int32, (ROWS, NL), 0)
    occ_sum = jnp.zeros((ROWS, NL), jnp.float32)
    for s in range(ROWS):
        occ_sum = jnp.where(row == s, occ[pairs[0, s]] + occ[pairs[1, s]], occ_sum)
    sig = jnp.broadcast_to(vir_row[...].reshape(1, NL), (ROWS, NL))

    turned_copy.wait()
    first = lax.axis_index("pair") * ROWS

    def assemble(s, carry):
        slot = lax.rem(partner[first + s], ROWS)
        q, j = lax.div(slot, 4), lax.rem(slot, 4)
        value = jnp.zeros((LAMS, NL), jnp.float32)
        for d in range(4):
            moved = pltpu.roll(decode(turned[d, q], 32), lax.rem(d + 4 - j, 4) * LAMS, 1)
            value = jnp.where(lane == d, moved, value)
        swapped[pl.ds(pl.multiple_of(s * LAMS, LAMS), LAMS), :] = value
        return carry

    lax.fori_loop(0, ROWS, assemble, 0, unroll=4)
    for copy in row_copies:
        copy.wait()

    def finish(lam, carry):
        cols = pl.ds(pl.multiple_of(lam * NL, NL), NL)
        symmetric = 0.5 * (own[:, cols] + swapped[pl.ds(lam, ROWS, stride=LAMS), :])
        denominator = (vir[lam_first + lam] + sig) - occ_sum
        amps = amplitudes[:, cols]
        value = other[:, cols] + symmetric - denominator * amps
        residual[:, cols] = value
        updated[:, cols] = amps + value / denominator
        return carry

    lax.fori_loop(0, LAMS, finish, 0)


def update(own, turned, partner, pair_list, occ_energy, vir_energy, amplitudes, other_terms):
    hbm = pl.BlockSpec(memory_space=pl.ANY)
    smem, vmem = pl.BlockSpec(memory_space=pltpu.SMEM), pl.BlockSpec(memory_space=pltpu.VMEM)
    shape = jax.ShapeDtypeStruct((ROWS, COLS), jnp.float32)
    return pl.pallas_call(
        update_kernel,
        out_shape=(shape, shape),
        in_specs=[hbm, hbm, smem, smem, smem, smem, vmem, hbm, hbm],
        out_specs=(vmem, vmem),
        scratch_shapes=[
            pltpu.VMEM((ROWS * LAMS, NL), jnp.float32),
            pltpu.VMEM((ROWS, COLS), jnp.float32),
            pltpu.VMEM((4, ROWS // 4, LAMS, NL), jnp.int16),
            pltpu.VMEM((ROWS, COLS), jnp.float32),
            pltpu.VMEM((ROWS, COLS), jnp.float32),
            pltpu.SemaphoreType.DMA((4,)),
        ],
        compiler_params=pltpu.CompilerParams(vmem_limit_bytes=60 << 20),
        cost_estimate=pl.CostEstimate(
            flops=8 * ROWS * COLS, bytes_accessed=3 << 20, transcendentals=0),
        name="update",
    )(own, turned, partner, pair_list.T, occ_energy, vir_energy, vir_energy, amplitudes, other_terms)


def local(
    amps_ao,
    integrals,
    tile_sizes,
    pair_list,
    partner,
    occ_energy,
    vir_energy,
    amplitudes,
    other_terms,
):
    own, turned = ladder_rows(amps_ao, integrals, tile_sizes)
    return update(own, turned, partner, pair_list, occ_energy, vir_energy, amplitudes, other_terms)


def solution(mesh):
    in_specs = (
        P("pair", None),
        P("pair", "ao"),
        P("pair"),
        P("pair", None),
        P(),
        P(),
        P(),
        P("pair", "ao"),
        P("pair", "ao"),
    )
    out_specs = (P("pair", "ao"), P("pair", "ao"))
    return jax.shard_map(local, mesh=mesh, in_specs=in_specs, out_specs=out_specs, check_vma=False)
```

```python
import functools

import jax
import jax.numpy as jnp
from jax import lax
from jax.experimental import pallas as pl
from jax.experimental.pallas import tpu as pltpu
from jax.sharding import PartitionSpec as P

NL = 128
TILE = 256
ROWS = 32
SLAB = 2048
QUARTER = SLAB // 4
COLS = 4096
LAMS = 32
C = 512
NK = COLS // 2 // C
LAGS = (1, 3, 5, 6)
MESH = pl.DeviceIdType.MESH

STEPS = 32760.0
OCTAVES = 20.17
FLOOR = 2.0**-12


def encode(value, slabs, twice=False):
    scale = jnp.where(twice, 0.5 / (FLOOR * slabs), 1.0 / (FLOOR * slabs))
    level = jnp.log2(1.0 + jnp.abs(value) * scale) * (STEPS / OCTAVES)
    level = jnp.where(value < 0.0, -level, level)
    return jnp.round(level).astype(jnp.int32).astype(jnp.int16)


def decode(code, slabs, twice=False):
    floor = jnp.where(twice, 2.0 * FLOOR * slabs, FLOOR * slabs)
    level = code.astype(jnp.int32).astype(jnp.float32)
    size = jnp.exp2(jnp.abs(level) * (OCTAVES / STEPS)) * floor - floor
    return jnp.where(level < 0.0, -size, size)


def ladder_kernel(
    amps, integrals, sizes, out, turned,
    a, b, staged, near, total, own1, keep, outz, inz, outo, ino, out1, in1, out2, in2, out3, in3, mask, rows3, out4, in4,
    b_sem, own_sem, here_sem, z_send, z_recv, plane_send, plane_recv, group_send, group_recv,
    sendz, recvz, sendo, recvo, send1, recv1, send2, recv2, send3, recv3, send4, recv4,
):
    pair, ao = lax.axis_index("pair"), lax.axis_index("ao")
    zh, y, x = pair // 16, (pair // 4) % 4, pair % 4
    zl, core = ao // 2, ao % 2
    mate = (pair, zl * 2 + 1 - core)
    beside = (pair, (1 - zl) * 2 + core)
    opposite = ((1 - zh) * 16 + y * 4 + x, (1 - zl) * 2 + core)
    across = ((1 - zh) * 16 + y * 4 + x, ao)

    def in_plane(i):
        return ((y + i // 4) % 4) * 4 + (x + i % 4) % 4

    def ring(part, j):
        if part == 0:
            return zh * 16 + y * 4 + (x + j) % 4, ao
        return zh * 16 + ((y + j) % 4) * 4 + x, ao

    def remote(src, dst, send, recv, device):
        return pltpu.make_async_remote_copy(
            src_ref=src, dst_ref=dst, send_sem=send, recv_sem=recv,
            device_id=device, device_id_type=MESH)

    def sent(ref, sem):
        remote(ref, ref, sem, sem, mate).wait_send()

    def received(ref, sem):
        remote(ref, ref, sem, sem, mate).wait_recv()

    def each(first, last, body):
        def step(i, carry):
            body(i)
            return carry

        lax.fori_loop(first, last, step, 0)

    barrier = pltpu.get_barrier_semaphore()

    def greet(peer):
        pl.semaphore_signal(barrier, inc=1, device_id=peer, device_id_type=MESH)

    each(1, 16, lambda i: greet((zh * 16 + in_plane(i), ao)))
    for peer in (opposite, across, *((pair, (ao + i) % 4) for i in range(1, 4))):
        greet(peer)
    pl.semaphore_wait(barrier, 20)

    def quarter_cols(quarter):
        return pl.ds(pl.multiple_of(quarter * QUARTER, QUARTER), QUARTER)

    def amp_cols(position, quarter):
        return amps.at[:, pl.ds(pl.multiple_of(position * SLAB + quarter * QUARTER, QUARTER), QUARTER)]

    def z_copy(i):
        return remote(
            amp_cols((1 - zh) * 16 + i, (1 - zl) * 2 + core), staged.at[i],
            z_send, z_recv, opposite)

    def plane_copy(h, i):
        there = in_plane(i)
        return remote(
            amp_cols(zh * 16 + there, ao) if h == 0 else staged.at[there],
            a.at[h, x, y, :, quarter_cols(ao)],
            plane_send.at[h], plane_recv.at[h, i % 4], (zh * 16 + there, ao))

    def group_copy(h, kind, g, quarter, device):
        block = a.at[h, (x + 4 - g) % 4, :, :, quarter_cols(quarter)]
        recv = group_recv.at[h, g if kind == 0 else 3 + kind]
        return remote(block, block, group_send.at[h], recv, device)

    def relay(h, g):
        column = a.at[h, (x + 4 - g) % 4, :, :, quarter_cols(ao)]
        received(column if g else column.at[pl.ds(0, 3)], plane_recv.at[h, g])

        def screen(i):
            rows = pl.ds(pl.multiple_of(i % 2 * 16, 16), 16)
            column[i // 2, rows, :] = column[i // 2, rows, :] * mask[:, quarter_cols(ao)]

        each(0, 2 * 4, screen)
        group_copy(h, 0, g, ao, beside).start()
        group_copy(h, 1, g, ao, mate).start()

    def relay_on(h, g):
        group_copy(h, 0, g, (1 - zl) * 2 + core, beside).wait_recv()
        group_copy(h, 2, g, (1 - zl) * 2 + core, mate).start()

    def relayed(h, kind):
        received(a.at[h, :, :, :, quarter_cols(0)], group_recv.at[h, 3 + kind])

    each(1, 16, lambda i: plane_copy(0, (i % 4) * 4 + i // 4).start())
    each(0, 16, lambda i: z_copy(i).start())
    own_copy = pltpu.make_async_copy(
        amp_cols(pair, ao), a.at[0, x, y, :, quarter_cols(ao)], own_sem)
    own_copy.start()

    def b_copy(t):
        cols = pl.ds(t * C, C)
        return pltpu.make_async_copy(integrals.at[:, cols], b.at[:, cols], b_sem.at[t])

    for k in range(NK):
        b_copy(k).start()
        b_copy(NK + k).start()

    lane = lax.broadcasted_iota(jnp.int32, (16, TILE), 1)
    for t in range(SLAB // TILE):
        mask[:, t * TILE:(t + 1) * TILE] = jnp.where(lane < sizes[t], 1.0, 0.0).astype(jnp.bfloat16)

    own_copy.wait()
    for g in range(4):
        relay(0, g)
    relayed(0, 1)

    def k_half(side):
        return pl.ds(pl.multiple_of(side * SLAB // 2, SLAB // 2), SLAB // 2)

    def half_product(h, t, side):
        return jnp.dot(
            a[h, :, :, :, k_half(side)].reshape(16 * ROWS, SLAB // 2),
            b[k_half(side), pl.ds(pl.multiple_of(t * C, C), C)],
            preferred_element_type=jnp.float32)

    def early(h, g):
        for t in (g, NK + g):
            if h == 0:
                b_copy(t).wait()
            near[t] = half_product(h, t, zl)
        relay_on(h, g)

    each(0, NK - 1, lambda g: early(0, g))
    received(staged, z_recv)
    each(1, 16, lambda i: plane_copy(1, (i % 4) * 4 + i // 4).start())
    here_copy = pltpu.make_async_copy(
        staged.at[y * 4 + x], a.at[1, x, y, :, quarter_cols(ao)], here_sem)
    here_copy.start()
    early(0, NK - 1)
    relayed(0, 2)

    def neighbour(t, side):
        along_x, along_y = ring(0, 1 + 2 * side)[0], ring(1, 1 + 2 * side)[0]
        return jnp.where(t // NK == 0, along_x, along_y), ao

    LAST = NK - 1

    def slot(h, t):
        return jnp.where(h == 0, t // NK * LAST + t % NK, 2 * LAST + t)

    def pair_slot(h, k):
        return jnp.where(h == 0, k, LAST + k)

    def copyo(s, t, side):
        return remote(
            outo.at[s, side], ino.at[s, side], sendo, recvo.at[s], neighbour(t, side))

    def copy1(s, t, side):
        return remote(
            out1.at[s, side], in1.at[s, side], send1, recv1.at[s], neighbour(t, side))

    def copy2(s, t, j):
        part = t // NK
        there = jnp.where(part == 0, ring(1, j + 1)[0], ring(0, j + 1)[0])
        return remote(out2.at[s, j], in2.at[s, j], send2, recv2.at[s], (there, ao))

    def copy3(h, k):
        to = (1 - h) * NK + k
        return remote(out3.at[pair_slot(h, k)], in3.at[to], send3, recv3.at[to], across)

    def copyz(part):
        return remote(outz.at[part], inz.at[part], sendz, recvz.at[part], across)

    def multiply(n):
        h, k = n // NK, n % NK
        for part in range(2):
            t = part * NK + k

            total[...] = (near[t] + half_product(h, t, 1 - zl)).reshape(4, 4, ROWS, C)
            here = x if part == 0 else y

            @pl.when(n == LAST)
            def _():
                def block(d):
                    outz[part, d] = encode(total[d], 1)

                each(0, 4, block)
                copyz(part).start()

            @pl.when(n == NK + LAST)
            def _():
                copyz(part).wait_recv()

                def block(d):
                    total[d] = total[d] + decode(inz[part, d], 1)

                each(0, 4, block)

            def block_of(d):
                block = total[d] if part == 0 else total[:, d]
                return block.reshape(4 * ROWS, C)

            @pl.when(n != LAST)
            def _():
                across_block = block_of((here + 2) % 4)
                s = slot(h, t)
                for side in range(2):
                    outo[s, side] = encode(
                        across_block[:, side * C // 2:(side + 1) * C // 2], 1, k == LAST)
                    copyo(s, t, side).start()
                for side in range(2):
                    keep[t, side] = block_of((here + 1 + 2 * side) % 4)
                own1[h, t] = block_of(here)

    def combine(h, t):
        s, twice = slot(h, t), t % NK == LAST
        received(ino.at[s], recvo.at[s])
        for side in range(2):
            half = slice(side * C // 2, (side + 1) * C // 2)
            rest = slice((1 - side) * C // 2, (2 - side) * C // 2)
            out1[s, side, :, half] = encode(
                keep[t, side, :, half] + decode(ino[s, side], 1, twice), 2, twice)
            out1[s, side, :, rest] = encode(keep[t, side, :, rest], 2, twice)
            copy1(s, t, side).start()

    def mine(t):
        return jnp.where(t // NK == 0, y, x)

    def rows_at(d):
        return pl.ds(pl.multiple_of(d * ROWS, ROWS), ROWS)

    def reduce1(h, t):
        s, twice = slot(h, t), t % NK == LAST
        received(in1.at[s], recv1.at[s])

        def summed(d):
            value = own1[h, t, rows_at(d), :]
            for side in range(2):
                value = value + decode(in1[s, side, rows_at(d), :], 2, twice)
            return value

        def push(j):
            out2[s, j] = encode(summed((mine(t) + j + 1) % 4), 4, twice)
            copy2(s, t, j).start()

        each(0, 3, push)
        own1[h, t, rows_at(mine(t)), :] = summed(mine(t))

    def reduce2(h, k):
        twice = k == LAST
        for part in range(2):
            t = part * NK + k
            s = slot(h, t)
            received(in2.at[s], recv2.at[s])
            value = own1[h, t, rows_at(mine(t)), :]
            for j in range(3):
                value = value + decode(in2[s, j], 4, twice)
            out3[pair_slot(h, k), part] = encode(value, 16, twice)
            own1[h, t, rows_at(mine(t)), :] = value
        copy3(h, k).start()

    def finish(k, last):
        received(in3.at[k], recv3.at[k])
        if not last:
            received(in3.at[NK + k], recv3.at[NK + k])
        for part in range(2):
            t = part * NK + k
            cols = pl.ds(pl.multiple_of(t * C, C), C)
            value = own1[1, t, rows_at(mine(t)), :]
            if last:
                out[:, cols] = decode(in3[k, part], 32)
            else:
                out[:, cols] = own1[0, t, rows_at(mine(t)), :] + decode(in3[k, part], 16)
                value = value + decode(in3[NK + k, part], 16)
            for l in range(C // NL):
                rows3[pl.ds(t * (C // NL) + l, ROWS, stride=LAMS), :] = (
                    value[:, l * NL:(l + 1) * NL])

    def both(k, body):
        body(k)
        body(NK + k)

    def step(n):
        def at(lag, body):
            @pl.when((n >= lag) & (n < lag + 2 * NK) & (n != lag + LAST))
            def _():
                body((n - lag) // NK, (n - lag) % NK)

        def tiles_at(lag, body):
            at(lag, lambda h, k: both(k, lambda t: body(h, t)))

        @pl.when((n < 2 * NK) & (n != NK))
        def _():
            multiply(n)

        @pl.when(n == 0)
        def _():
            here_copy.wait()
            for g in range(4):
                relay(1, g)

        tiles_at(LAGS[0], combine)
        tiles_at(LAGS[1], reduce1)
        at(LAGS[2], reduce2)

        @pl.when((n >= NK + LAGS[3]) & (n < NK + LAGS[3] + LAST))
        def _():
            finish(n - NK - LAGS[3], False)

        @pl.when(n == NK)
        def _():
            relayed(1, 1)
            each(0, NK, lambda g: early(1, g))
            relayed(1, 2)
            multiply(n)

    each(0, NK + max(LAGS[3] + LAST, LAGS[2] + NK), step)
    finish(LAST, True)

    def turn(q):
        block = rows3[pl.ds(pl.multiple_of(q * NL, NL), NL), :].T
        for d in range(4):
            out4[d, q] = encode(block[d * LAMS:(d + 1) * LAMS], 32)

    each(0, ROWS // 4, turn)

    def copy4(i):
        to = (ao + i) % 4
        return remote(out4.at[to], in4.at[3 - i], send4, recv4, (pair, to))

    for i in range(1, 4):
        copy4(i).start()
    turned[ao] = out4[ao]

    sent(staged, z_send)
    for h in range(2):
        sent(staged.at[pl.ds(0, 15)], plane_send.at[h])
        sent(a.at[h, :, :, :, pl.ds(0, 3 * QUARTER)], group_send.at[h])
    for ref, sem in (
        (outo, sendo), (out1, send1), (out2, send2), (out3, send3), (outz, sendz),
        (out4.at[pl.ds(0, 3)], send4),
    ):
        sent(ref, sem)
    received(in4, recv4)
    for i in range(1, 4):
        turned[(ao + 4 - i) % 4] = in4[3 - i]


def ladder_rows(amps_ao, integrals, tile_sizes):
    sem = pltpu.SemaphoreType.DMA
    vmem = pltpu.VMEM
    tiles, slots = 2 * NK, 4 * NK - 2
    return pl.pallas_call(
        ladder_kernel,
        out_shape=(
            jax.ShapeDtypeStruct((ROWS, COLS), jnp.float32),
            jax.ShapeDtypeStruct((4, ROWS // 4, LAMS, NL), jnp.int16),
        ),
        in_specs=[
            pl.BlockSpec(memory_space=pl.ANY),
            pl.BlockSpec(memory_space=pl.ANY),
            pl.BlockSpec(memory_space=pltpu.SMEM),
        ],
        out_specs=(pl.BlockSpec(memory_space=pltpu.VMEM), pl.BlockSpec(memory_space=pltpu.VMEM)),
        scratch_shapes=[
            vmem((2, 4, 4, ROWS, SLAB), jnp.bfloat16),
            vmem((SLAB, COLS), jnp.bfloat16),
            vmem((16, ROWS, QUARTER), jnp.bfloat16),
            vmem((tiles, 16 * ROWS, C), jnp.float32),
            vmem((4, 4, ROWS, C), jnp.float32),
            vmem((2, tiles, 4 * ROWS, C), jnp.float32),
            vmem((tiles, 2, 4 * ROWS, C), jnp.float32),
            vmem((2, 4, 4, ROWS, C), jnp.int16),
            vmem((2, 4, 4, ROWS, C), jnp.int16),
            vmem((slots, 2, 4 * ROWS, C // 2), jnp.int16),
            vmem((slots, 2, 4 * ROWS, C // 2), jnp.int16),
            vmem((slots, 2, 4 * ROWS, C), jnp.int16),
            vmem((slots, 2, 4 * ROWS, C), jnp.int16),
            vmem((slots, 3, ROWS, C), jnp.int16),
            vmem((slots, 3, ROWS, C), jnp.int16),
            vmem((slots // 2, 2, ROWS, C), jnp.int16),
            vmem((tiles, 2, ROWS, C), jnp.int16),
            vmem((16, SLAB), jnp.bfloat16),
            vmem((ROWS * LAMS + LAMS, NL), jnp.float32),
            vmem((4, ROWS // 4, LAMS, NL), jnp.int16),
            vmem((3, ROWS // 4, LAMS, NL), jnp.int16),
            sem((tiles,)), sem, sem, sem, sem, sem((2,)), sem((2, 4)), sem((2,)), sem((2, 6)),
            sem, sem((2,)), sem, sem((slots,)), sem, sem((slots,)), sem, sem((slots,)),
            sem, sem((tiles,)), sem, sem,
        ],
        compiler_params=pltpu.CompilerParams(
            collective_id=0, has_side_effects=True, vmem_limit_bytes=60 << 20),
        cost_estimate=pl.CostEstimate(
            flops=2 * 1024 * SLAB * COLS, bytes_accessed=24 << 20, transcendentals=0),
        name="ladder",
    )(amps_ao, integrals, tile_sizes)


def update_kernel(
    own_hbm, turned_hbm, partner, pairs, occ, vir, vir_row, amplitudes_hbm, other_hbm,
    residual, updated, swapped, own, turned, amplitudes, other, sem
):
    turned_copy = pltpu.make_async_copy(turned_hbm, turned, sem.at[0])
    row_copies = [
        pltpu.make_async_copy(src, dst, sem.at[i + 1])
        for i, (src, dst) in enumerate(
            ((own_hbm, own), (amplitudes_hbm, amplitudes), (other_hbm, other)))]
    turned_copy.start()
    for copy in row_copies:
        copy.start()
    lam_first = lax.axis_index("ao") * LAMS
    lane = lax.broadcasted_iota(jnp.int32, (LAMS, NL), 1) // LAMS

    row = lax.broadcasted_iota(jnp.int32, (ROWS, NL), 0)
    occ_sum = jnp.zeros((ROWS, NL), jnp.float32)
    for s in range(ROWS):
        occ_sum = jnp.where(row == s, occ[pairs[0, s]] + occ[pairs[1, s]], occ_sum)
    sig = jnp.broadcast_to(vir_row[...].reshape(1, NL), (ROWS, NL))

    turned_copy.wait()
    first = lax.axis_index("pair") * ROWS

    def assemble(s, carry):
        slot = lax.rem(partner[first + s], ROWS)
        q, j = lax.div(slot, 4), lax.rem(slot, 4)
        value = jnp.zeros((LAMS, NL), jnp.float32)
        for d in range(4):
            moved = pltpu.roll(decode(turned[d, q], 32), lax.rem(d + 4 - j, 4) * LAMS, 1)
            value = jnp.where(lane == d, moved, value)
        swapped[pl.ds(pl.multiple_of(s * LAMS, LAMS), LAMS), :] = value
        return carry

    lax.fori_loop(0, ROWS, assemble, 0, unroll=4)
    for copy in row_copies:
        copy.wait()

    def finish(lam, carry):
        cols = pl.ds(pl.multiple_of(lam * NL, NL), NL)
        symmetric = 0.5 * (own[:, cols] + swapped[pl.ds(lam, ROWS, stride=LAMS), :])
        denominator = (vir[lam_first + lam] + sig) - occ_sum
        amps = amplitudes[:, cols]
        value = other[:, cols] + symmetric - denominator * amps
        residual[:, cols] = value
        updated[:, cols] = amps + value / denominator
        return carry

    lax.fori_loop(0, LAMS, finish, 0)


def update(own, turned, partner, pair_list, occ_energy, vir_energy, amplitudes, other_terms):
    hbm = pl.BlockSpec(memory_space=pl.ANY)
    smem, vmem = pl.BlockSpec(memory_space=pltpu.SMEM), pl.BlockSpec(memory_space=pltpu.VMEM)
    shape = jax.ShapeDtypeStruct((ROWS, COLS), jnp.float32)
    return pl.pallas_call(
        update_kernel,
        out_shape=(shape, shape),
        in_specs=[hbm, hbm, smem, smem, smem, smem, vmem, hbm, hbm],
        out_specs=(vmem, vmem),
        scratch_shapes=[
            pltpu.VMEM((ROWS * LAMS + LAMS, NL), jnp.float32),
            pltpu.VMEM((ROWS, COLS), jnp.float32),
            pltpu.VMEM((4, ROWS // 4, LAMS, NL), jnp.int16),
            pltpu.VMEM((ROWS, COLS), jnp.float32),
            pltpu.VMEM((ROWS, COLS), jnp.float32),
            pltpu.SemaphoreType.DMA((4,)),
        ],
        compiler_params=pltpu.CompilerParams(vmem_limit_bytes=60 << 20),
        cost_estimate=pl.CostEstimate(
            flops=8 * ROWS * COLS, bytes_accessed=3 << 20, transcendentals=0),
        name="update",
    )(own, turned, partner, pair_list.T, occ_energy, vir_energy, vir_energy, amplitudes, other_terms)


def local(
    amps_ao,
    integrals,
    tile_sizes,
    pair_list,
    partner,
    occ_energy,
    vir_energy,
    amplitudes,
    other_terms,
):
    own, turned = ladder_rows(amps_ao, integrals, tile_sizes)
    return update(own, turned, partner, pair_list, occ_energy, vir_energy, amplitudes, other_terms)


def solution(mesh):
    in_specs = (
        P("pair", None),
        P("pair", "ao"),
        P("pair"),
        P("pair", None),
        P(),
        P(),
        P(),
        P("pair", "ao"),
        P("pair", "ao"),
    )
    out_specs = (P("pair", "ao"), P("pair", "ao"))
    return jax.shard_map(local, mesh=mesh, in_specs=in_specs, out_specs=out_specs, check_vma=False)
```
